256 devices in a mesh: inner: 8 (over y, z_lo), outer: 8 (over z_hi, core), tensor: 4 (over x).
Axes of the slice: x: 4, y: 4, z: 8 (z_hi: 4, z_lo: 2; z = z_hi * 2 + z_lo), core: 2. Of those that a mesh axis runs over, the one named last changes fastest.
Arguments:
- query_matrix: bfloat16 [8192, 4096], P(('inner', 'outer'), 'tensor'), may hold values from -6 to 6
- key_matrix: bfloat16 [8192, 512], P(('inner', 'outer'), 'tensor'), may hold values from -6 to 6
- value_matrix: bfloat16 [8192, 512], P(('inner', 'outer'), 'tensor'), may hold values from -12 to 12
- segment_ids: int32 [8192], replicated, may hold values from 0 to 7, never falling along the last dimension, each value on 1 to 4096 neighbouring positions
- block_order: int32 [128], replicated, may hold values from 0 to 127, each once
- out_weight: bfloat16 [4096, 4096], P('tensor'), may hold values from -0.09375 to 0.09375
- d_attended: bfloat16 [8192, 4096], P(('inner', 'outer', 'tensor')), may hold values from -6 to 6
Outputs:
- attended: bfloat16 [8192, 4096], P(('inner', 'outer'), 'tensor')
- d_queries: bfloat16 [8192, 4096], P(('inner', 'outer'), 'tensor')
- key_gradient: bfloat16 [8192, 512], P(('inner', 'outer'), 'tensor')
- value_gradient: bfloat16 [8192, 512], P(('inner', 'outer'), 'tensor')
The draws below stay inside these ranges and needn't reach their ends.
Inputs may be any that keep to these rules, and one draw needn't show every extreme that they name: `segment_ids`: never falls along the sequence position; each of the 8 documents holds one or more positions, at most half of 8192, and one holds exactly half of 8192. `block_order`: each of the 128 blocks exactly once.
All inputs are finite; a program needn't handle non-finite values.
Results may differ from the reference program's by a relative error of at most 0.019.
Values may be sent and summed in bfloat16 or wider, within the bound.
A program may use at most 128 MiB of HBM per device.

```python
import math
import jax
import jax.numpy as jnp
import numpy as np
from jax import lax

HQ = 32
KEY_HEADS = 4
HEAD_FEATURES = 128
DW = 4096
DOCS = 8
QUERY_PER_KEY = 8
SPAN = 64
TOKEN_LENGTH = 8192
SPANS = 128


def draw_query_matrix(key, part):
    key = jax.random.fold_in(key, 5)
    final_output = jnp.clip(2.0 * jax.random.normal(key, (TOKEN_LENGTH, HQ * HEAD_FEATURES)), -6.0, 6.0)
    return final_output.astype(jnp.bfloat16)


def draw_key_matrix(key, part):
    key = jax.random.fold_in(key, 9)
    final_output = jnp.clip(jax.random.normal(key, (TOKEN_LENGTH, KEY_HEADS * HEAD_FEATURES)), -4.0, 4.0)
    return final_output.astype(jnp.bfloat16)


def shard_levels(own_key, extent, cuts, low, largest):
    gain, own = 1.0, jax.random.fold_in(own_key, 6)
    for axis_at, parts in cuts:
        steps = jnp.exp(jax.random.uniform(jax.random.fold_in(own, axis_at), (parts,), jnp.float32, low / len(cuts), largest / len(cuts)))
        gain = gain * jnp.repeat(steps, extent[axis_at] // parts).reshape([-1 if axis == axis_at else 1 for axis in range(len(extent))])
    return gain


def split_up(count, total, reach, lean):
    weights = [(1 << 20) // math.isqrt(rank ** lean) + 1 for rank in range(2, count + 1)]
    surplus, counts = total - reach - (count - 1), [1] * (count - 1)
    while surplus > 0:
        movable = [i for i in range(count - 1) if counts[i] < reach]
        whole, budget = sum([weights[i] for i in movable]), surplus
        for i in movable:
            addition = min(reach - counts[i], max(1, budget * weights[i] // whole), surplus)
            counts[i] = counts[i] + addition
            surplus = surplus - addition
    return np.array([reach] + counts)


def ragged(rng, count, total, most, skew):
    if count == 2:
        one = jax.random.randint(rng, (), max(1, total - most), min(most, total - 1) + 1)
        return jnp.stack([one, total - one])
    tallies = jnp.asarray(split_up(count, total, most, skew), jnp.int32)
    pairs = (count - 1) // 2
    giver, taker = tallies[1:1 + 2 * pairs:2], tallies[2:2 + 2 * pairs:2]
    room = jnp.minimum(giver - 1, most - taker)
    shifted = jax.random.randint(jax.random.fold_in(rng, 1), (pairs,), 0, 1 << 20) % (room + 1)
    tallies = tallies.at[1:1 + 2 * pairs:2].set(giver - shifted).at[2:2 + 2 * pairs:2].set(taker + shifted)
    return tallies[jax.random.permutation(jax.random.fold_in(rng, 2), count)]


def centred(stream_key, shape, deviation, reach, cuts=(), kind=jnp.bfloat16):
    result = jax.random.normal(stream_key, shape, jnp.float32) * deviation
    if len(cuts) > 0:
        result = shard_levels(stream_key, shape, cuts, -0.22, 0.18) * result
    return jnp.clip(result, min=-reach, max=reach).astype(kind)


def setup_inputs(seed: int = 0) -> dict:
    streams_of = jax.random.split(jax.random.key(seed), 8)
    query_matrix = draw_query_matrix(jax.random.fold_in(streams_of[7], 71), 0)
    key_matrix = draw_key_matrix(jax.random.fold_in(streams_of[7], 71), 0)
    value_matrix = centred(streams_of[2], (TOKEN_LENGTH, KEY_HEADS * HEAD_FEATURES), 3.0, 12.0, ((0, 64), (1, 4)))
    segment_ids = jnp.searchsorted(jnp.cumsum(ragged(streams_of[3], DOCS, TOKEN_LENGTH, TOKEN_LENGTH // 2, 2)), jnp.arange(TOKEN_LENGTH), side="right").astype(jnp.int32)
    block_order = jax.random.permutation(streams_of[4], SPANS).astype(jnp.int32)
    out_weight = centred(streams_of[5], (HQ * HEAD_FEATURES, DW), (HQ * HEAD_FEATURES) ** -0.5, 0.09375, ((0, 4),))
    d_attended = centred(streams_of[6], (TOKEN_LENGTH, DW), 1.0, 6.0, ((0, 256),))
    return {"query_matrix": query_matrix, "key_matrix": key_matrix, "value_matrix": value_matrix, "segment_ids": segment_ids, "block_order": block_order, "out_weight": out_weight, "d_attended": d_attended}


def rounded(tensor):
    return lax.optimization_barrier(tensor.astype(jnp.bfloat16)).astype(jnp.float32)

def token_places(segment_ids, block_order):
    row_ids = jnp.arange(TOKEN_LENGTH, dtype=jnp.int32)
    places = block_order[row_ids // SPAN] * SPAN + row_ids % SPAN
    return (places, segment_ids[places])

def reference(query_matrix, key_matrix, value_matrix, segment_ids, block_order, out_weight, d_attended):
    softmax_scale = 1.0 / math.sqrt(HEAD_FEATURES)
    places, documents = token_places(segment_ids, block_order)
    attention_gradient = jnp.dot(d_attended, out_weight.T, preferred_element_type=jnp.float32).astype(jnp.bfloat16)
    heads_of_keys = key_matrix.astype(jnp.float32).reshape(TOKEN_LENGTH, KEY_HEADS, HEAD_FEATURES)
    heads_of_values = value_matrix.astype(jnp.float32).reshape(TOKEN_LENGTH, KEY_HEADS, HEAD_FEATURES)
    rows_per_block = 128

    def one_block(carried, block_index):
        key_sum, value_sum = carried
        starting_row = (block_index * rows_per_block).astype(jnp.int32)
        block_of_queries = lax.dynamic_slice_in_dim(query_matrix, starting_row, rows_per_block, 0).astype(jnp.float32).reshape(rows_per_block, KEY_HEADS, QUERY_PER_KEY, HEAD_FEATURES)
        gradient_block = lax.dynamic_slice_in_dim(attention_gradient, starting_row, rows_per_block, 0).astype(jnp.float32).reshape(rows_per_block, KEY_HEADS, QUERY_PER_KEY, HEAD_FEATURES)
        own_places = lax.dynamic_slice_in_dim(places, starting_row, rows_per_block, 0)
        own_docs = lax.dynamic_slice_in_dim(documents, starting_row, rows_per_block, 0)
        visible = (places[None, :] <= own_places[:, None]) & (documents[None, :] == own_docs[:, None])
        scores = jnp.einsum('qagd,kad->agqk', block_of_queries, heads_of_keys) * softmax_scale
        scores = jnp.where(visible, scores, -1e+30)
        row_max = lax.optimization_barrier(jnp.max(scores, axis=-1, keepdims=True))
        exponent = jnp.where(visible, jnp.exp(scores - row_max), 0.0)
        row_sum = lax.optimization_barrier(jnp.sum(exponent, axis=-1, keepdims=True))
        weights = rounded(exponent)
        mixed_values = jnp.einsum('agqk,kad->qagd', weights, heads_of_values) / jnp.transpose(row_sum, (2, 0, 1, 3))
        attended = lax.optimization_barrier(mixed_values.astype(jnp.bfloat16))
        row_delta = jnp.einsum('qagd,qagd->agq', gradient_block, attended.astype(jnp.float32))[..., None]
        normed = weights / row_sum
        prob_b = rounded(normed)
        d_prob = jnp.einsum('qagd,kad->agqk', gradient_block, heads_of_values)
        d_score = rounded(normed * (d_prob - row_delta))
        d_query = (jnp.einsum('agqk,kad->qagd', d_score, heads_of_keys) * softmax_scale).astype(jnp.bfloat16)
        key_sum = key_sum + jnp.einsum('agqk,qagd->kad', d_score, block_of_queries)
        value_sum = value_sum + jnp.einsum('agqk,qagd->kad', prob_b, gradient_block)
        return ((key_sum, value_sum), (attended.reshape(rows_per_block, HQ * HEAD_FEATURES), d_query.reshape(rows_per_block, HQ * HEAD_FEATURES)))
    zeroed_sums = jnp.zeros((TOKEN_LENGTH, KEY_HEADS, HEAD_FEATURES), jnp.float32)
    gradient_sums, blocks = lax.scan(one_block, (zeroed_sums, zeroed_sums), jnp.arange(TOKEN_LENGTH // rows_per_block, dtype=jnp.int32))
    attended = blocks[0].reshape(TOKEN_LENGTH, HQ * HEAD_FEATURES)
    d_queries = blocks[1].reshape(TOKEN_LENGTH, HQ * HEAD_FEATURES)
    key_gradient = (gradient_sums[0] * softmax_scale).astype(jnp.bfloat16).reshape(TOKEN_LENGTH, KEY_HEADS * HEAD_FEATURES)
    value_gradient = gradient_sums[1].astype(jnp.bfloat16).reshape(TOKEN_LENGTH, KEY_HEADS * HEAD_FEATURES)
    return (attended, d_queries, key_gradient, value_gradient)
```

```python
import functools
import math

import jax
import jax.numpy as jnp
from jax import lax
from jax.experimental import pallas as pl
from jax.experimental.pallas import tpu as pltpu
from jax.sharding import PartitionSpec as P

D = 128
HEADS = 8
ROWS = 128
SPAN = 64
SPANS = 128
TOKENS = 8192
QROWS = SPAN * HEADS
TILE_SPANS = 8
TILE = TILE_SPANS * SPAN
MAX_TILES = 65 // TILE_SPANS + 1
SCALE = 1.0 / math.sqrt(D)
EXP2_SCALE = SCALE * math.log2(math.e)
F32 = jnp.float32
BF16 = jnp.bfloat16
MESH = pl.DeviceIdType.MESH
VMEM = pl.BlockSpec(memory_space=pltpu.VMEM)
SMEM = pl.BlockSpec(memory_space=pltpu.SMEM)
ANY = pl.BlockSpec(memory_space=pl.ANY)
LIMIT = 56 * 1024 * 1024
PIECES = (4, 2, 4, 2, ROWS, 2 * D)


class Place:
    def __init__(self):
        inner, outer = lax.axis_index("inner"), lax.axis_index("outer")
        self.x = lax.axis_index("tensor")
        self.y = lax.div(inner, 2)
        self.core = lax.rem(outer, 2)
        z = lax.div(outer, 2) * 2 + lax.rem(inner, 2)
        self.ys = [lax.rem(self.y + s, 4) for s in range(4)]
        self.xs = [lax.rem(self.x + s, 4) for s in range(4)]
        zs = [lax.rem(z + s, 8) for s in range(8)]
        self.zs = [(at, lax.rem(at, 2), lax.div(at, 2)) for at in zs]
        self.z = self.zs[0]

    def dy(self, step):
        return self.ys[step % 4]

    def dz(self, step):
        return self.zs[step % 8]

    def dx(self, step):
        return self.xs[step % 4]

    def device(self, y=None, z=None, core=None, x=None):
        y = self.y if y is None else y
        z = self.z if z is None else z
        core = self.core if core is None else core
        x = self.x if x is None else x
        return (y * 2 + z[1], z[2] * 2 + core, x)

    def greet(self, devices):
        barrier = pltpu.get_barrier_semaphore()
        for device in devices:
            pl.semaphore_signal(barrier, inc=1, device_id=device, device_id_type=MESH)
        pl.semaphore_wait(barrier, len(devices))


class Sends:
    def __init__(self, sems):
        self.sems, self.copies = sems, []

    def __call__(self, src, dst, recv_sem, device):
        copy = pltpu.make_async_remote_copy(
            src_ref=src, dst_ref=dst, send_sem=self.sems.at[len(self.copies)],
            recv_sem=recv_sem, device_id=device, device_id_type=MESH,
        )
        copy.start()
        self.copies.append(copy)

    def wait(self):
        for copy in self.copies:
            copy.wait_send()
        self.copies = []


def arrived(ref, send_sem, recv_sem, device):
    pltpu.make_async_remote_copy(
        src_ref=ref, dst_ref=ref, send_sem=send_sem, recv_sem=recv_sem,
        device_id=device, device_id_type=MESH,
    ).wait_recv()


def piece(ref, y, z, *core):
    return ref.at[(y, z[1], z[2]) + core]


def gather_kernel(
    k_ref, v_ref, da_ref, w_ref, kv_ref, g_ref,
    own, da_all, w_all, local_sem, send_sem, recv_sem, mate_send, mate_recv, x_send, x_recv,
):
    me = Place()
    y, z, x = me.y, me.z, me.x
    w_copy = pltpu.make_async_copy(w_ref, w_all, local_sem.at[0])
    w_copy.start()
    own[:, :D] = k_ref[...]
    own[:, D:] = v_ref[...]
    own_copy = pltpu.make_async_copy(own, piece(kv_ref, y, z, me.core), local_sem.at[1])
    own_copy.start()
    da_all[x] = da_ref[...]
    mate = me.device(core=1 - me.core)
    me.greet(
        [mate]
        + [me.device(y=me.dy(s)) for s in (1, -1, 2)]
        + [me.device(z=me.dz(s)) for s in (1, -1)]
        + [me.device(x=me.dx(s)) for s in (1, -1)]
    )
    up_x, down_x = me.device(x=me.dx(1)), me.device(x=me.dx(-1))
    half = da_ref.shape[1] // 2
    x_sends = Sends(x_send)

    def x_start():
        x_sends(da_ref, da_all.at[x], x_recv.at[0], up_x)
        x_sends(da_ref, da_all.at[x], x_recv.at[1], down_x)

    def x_middle():
        low, high = me.dx(-1), me.dx(1)
        arrived(da_all.at[low], x_send.at[0], x_recv.at[0], mate)
        part = da_all.at[low, :, pl.ds(0, half)]
        x_sends(part, part, x_recv.at[2], up_x)
        arrived(da_all.at[high], x_send.at[0], x_recv.at[1], mate)
        part = da_all.at[high, :, pl.ds(half, half)]
        x_sends(part, part, x_recv.at[3], down_x)

    def x_end():
        far = me.dx(2)
        arrived(da_all.at[far, :, pl.ds(0, half)], x_send.at[0], x_recv.at[2], mate)
        arrived(da_all.at[far, :, pl.ds(half, half)], x_send.at[0], x_recv.at[3], mate)
        w_copy.wait()

    def product(at):
        width = 256
        rows = da_all[...].reshape(ROWS, da_ref.shape[1])
        g_ref[:, at * width:(at + 1) * width] = lax.dot_general(
            rows, w_all[at * width:(at + 1) * width, :], (((1,), (1,)), ((), ())),
            preferred_element_type=F32,
        ).astype(BF16)

    def to_mate(src, dst):
        pltpu.make_async_remote_copy(
            src_ref=src, dst_ref=dst, send_sem=mate_send, recv_sem=mate_recv,
            device_id=mate, device_id_type=MESH,
        ).start()

    def finish(core, sends):
        theirs = kv_ref.at[:, :, :, 1 - core]
        ours = kv_ref.at[:, :, :, core]
        arrived(theirs, mate_send, mate_recv, mate)
        pltpu.make_async_remote_copy(
            src_ref=ours, dst_ref=ours, send_sem=mate_send, recv_sem=mate_recv,
            device_id=mate, device_id_type=MESH,
        ).wait_send()
        sends.wait()
        x_sends.wait()

    up_z, down_z = me.device(z=me.dz(1)), me.device(z=me.dz(-1))
    up_y, down_y = me.device(y=me.dy(1)), me.device(y=me.dy(-1))

    def fetch(core, sends, step_y, step_z, devices, wait=True):
        py, pz = me.dy(step_y), me.dz(step_z)
        dst = piece(kv_ref, py, pz, core)
        sem = recv_sem.at[py * 8 + pz[0]]
        src = dst if wait else own
        if wait:
            arrived(dst, mate_send, sem, mate)
        for device in devices:
            sends(src, dst, sem, device)
        to_mate(src, dst)

    @pl.when(me.core == 0)
    def _():
        sends = Sends(send_sem)
        fetch(0, sends, 0, 0, [up_y, down_y, me.device(y=me.dy(2)), up_z, down_z], wait=False)
        x_start()
        for i in (1, -1, 2):
            fetch(0, sends, i, 0, [up_z, down_z])
        for s in (1, 2, 3):
            for i in (0, 1, -1, 2):
                fetch(0, sends, i, -s, [up_z] if s < 3 or i in (0, 1) else [])
                fetch(0, sends, i, s, [down_z] if s < 3 or i in (-1, 2) else [])
            if s == 2:
                x_middle()
        x_end()
        for at, i in enumerate((0, -1, 1, 2)):
            product(at)
            fetch(0, sends, i, 4, [])
        finish(0, sends)

    @pl.when(me.core == 1)
    def _():
        sends = Sends(send_sem)
        fetch(1, sends, 0, 0, [up_z, down_z, up_y, down_y], wait=False)
        x_start()

        def across(s):
            fetch(1, sends, -1, s, [up_y] if s <= 0 else [])
            fetch(1, sends, 1, s, [down_y] if s > 0 else [])

        for s in (1, 2, 3):
            fetch(1, sends, 0, -s, [up_z, up_y, down_y])
            fetch(1, sends, 0, s, ([down_z] if s < 3 else []) + [up_y, down_y])
            for r in ((0,) if s == 1 else (1 - s, s - 1)):
                across(r)
        fetch(1, sends, 0, 4, [up_y, down_y])
        x_middle()
        across(-3)
        across(3)
        across(4)
        x_end()
        for at in range(4):
            product(at)
            for s in ((0, -1), (1, -2), (2, -3), (3, 4))[at]:
                fetch(1, sends, 2, s, [])
        finish(1, sends)

    own_copy.wait()


def gather(k, v, da, w):
    return pl.pallas_call(
        gather_kernel,
        out_shape=(
            jax.ShapeDtypeStruct(PIECES, BF16),
            jax.ShapeDtypeStruct((ROWS, w.shape[0]), BF16),
        ),
        in_specs=[VMEM, VMEM, VMEM, ANY],
        out_specs=(ANY, VMEM),
        scratch_shapes=[
            pltpu.VMEM((ROWS, 2 * D), BF16),
            pltpu.VMEM((4,) + da.shape, BF16),
            pltpu.VMEM(w.shape, BF16),
            pltpu.SemaphoreType.DMA((2,)),
            pltpu.SemaphoreType.DMA((48,)),
            pltpu.SemaphoreType.DMA((32,)),
            pltpu.SemaphoreType.DMA,
            pltpu.SemaphoreType.DMA,
            pltpu.SemaphoreType.DMA((4,)),
            pltpu.SemaphoreType.DMA((4,)),
        ],
        compiler_params=pltpu.CompilerParams(
            collective_id=0, has_side_effects=True, vmem_limit_bytes=LIMIT
        ),
        name="gather",
    )(k, v, da, w)


def attention_kernel(
    seq_ref, order_ref, seg_ref, q_ref, g_ref, kv_ref, o_ref, dq_ref, dkv_ref,
    stored, qs, gs, q_t, g_t, weights, maxima, acc,
):
    seq = seq_ref[0]
    dkv_ref[...] = jnp.zeros_like(dkv_ref)
    for r in range(SPANS):
        stored[order_ref[r]] = r
    seg = seg_ref[...]
    starts = [jnp.sum((seg < d).astype(jnp.int32)) for d in range(1, 8)]
    key_iota = lax.broadcasted_iota(jnp.int32, (TILE, QROWS), 0)
    lane = lax.broadcasted_iota(jnp.int32, (1, QROWS), 1)

    def begin(position):
        first = jnp.zeros_like(position)
        for start in starts:
            first = jnp.maximum(first, jnp.where(start <= position, start, 0))
        return first

    def one_span(half, _):
        row = pl.multiple_of(half * SPAN, SPAN)
        span = order_ref[seq * 2 + half]
        position = span * SPAN + lax.rem(lane, SPAN)
        first = begin(position)
        span_0 = lax.div(begin(span * SPAN), SPAN)
        tiles = lax.div(span - span_0 + TILE_SPANS, TILE_SPANS)
        for h in range(HEADS):
            qs[h * SPAN:(h + 1) * SPAN, :] = q_ref[pl.ds(row, SPAN), h * D:(h + 1) * D]
            gs[h * SPAN:(h + 1) * SPAN, :] = g_ref[pl.ds(row, SPAN), h * D:(h + 1) * D]
        q_t[...] = qs[...].T
        g_t[...] = gs[...].T

        def rows_of(tile):
            return [
                pl.multiple_of(
                    stored[jnp.minimum(span_0 + tile * TILE_SPANS + b, SPANS - 1)] * SPAN, SPAN
                )
                for b in range(TILE_SPANS)
            ]

        def load(rows, column):
            return jnp.concatenate(
                [kv_ref[pl.ds(r, SPAN), column * D:(column + 1) * D] for r in rows], axis=0
            )

        acc[...] = jnp.zeros_like(acc)

        def forward(tile, carried):
            top, total = carried
            rows = rows_of(tile)
            scores = jnp.dot(load(rows, 0), q_t[...], preferred_element_type=F32)
            place = key_iota + (span_0 + tile * TILE_SPANS) * SPAN
            scores = jnp.where((place >= first) & (place <= position), scores, -1e30)
            new = jnp.maximum(top, jnp.max(scores, axis=0, keepdims=True))
            shrink = jnp.exp2((top - new) * EXP2_SCALE)
            exponent = jnp.exp2((scores - new) * EXP2_SCALE)
            total = total * shrink + jnp.sum(exponent, axis=0, keepdims=True)
            rounded = exponent.astype(BF16)
            weights[tile] = rounded
            maxima[tile] = new
            acc[...] = acc[...] * shrink + lax.dot_general(
                load(rows, 1), rounded, (((0,), (0,)), ((), ())), preferred_element_type=F32
            )
            return new, total

        top, total = lax.fori_loop(
            0, tiles, forward,
            (jnp.full((1, QROWS), -1e30, F32), jnp.zeros((1, QROWS), F32)),
        )
        inverse = 1.0 / total
        attended_t = (acc[...] * inverse).astype(BF16)
        delta = jnp.sum(
            attended_t.astype(F32) * g_t[...].astype(F32), axis=0, keepdims=True
        )
        attended = attended_t.T
        for h in range(HEADS):
            o_ref[pl.ds(row, SPAN), h * D:(h + 1) * D] = attended[h * SPAN:(h + 1) * SPAN, :]
        acc[...] = jnp.zeros_like(acc)

        def backward(tile, _):
            rows = rows_of(tile)
            factor = jnp.exp2((maxima[tile] - top) * EXP2_SCALE) * inverse
            d_prob = jnp.dot(load(rows, 1), g_t[...], preferred_element_type=F32)
            normed = weights[tile].astype(F32) * factor
            d_score = (normed * (d_prob - delta)).astype(BF16)
            acc[...] += lax.dot_general(
                load(rows, 0), d_score, (((0,), (0,)), ((), ())), preferred_element_type=F32
            )
            dk = jnp.dot(d_score, qs[...], preferred_element_type=F32)
            dv = jnp.dot(normed.astype(BF16), gs[...], preferred_element_type=F32)
            for b, r in enumerate(rows):
                for column, terms in enumerate((dk, dv)):
                    at = (pl.ds(r, SPAN), slice(column * D, (column + 1) * D))
                    dkv_ref[at] = (
                        dkv_ref[at].astype(F32) + terms[b * SPAN:(b + 1) * SPAN, :]
                    ).astype(BF16)
            return 0

        lax.fori_loop(0, tiles, backward, 0)
        dq = (acc[...] * SCALE).astype(BF16).T
        for h in range(HEADS):
            dq_ref[pl.ds(row, SPAN), h * D:(h + 1) * D] = dq[h * SPAN:(h + 1) * SPAN, :]
        return 0

    lax.fori_loop(0, 2, one_span, 0)


def attention(seq, order, seg, q, g, kv):
    return pl.pallas_call(
        attention_kernel,
        out_shape=(
            jax.ShapeDtypeStruct(q.shape, BF16),
            jax.ShapeDtypeStruct(q.shape, BF16),
            jax.ShapeDtypeStruct(kv.shape, BF16),
        ),
        in_specs=[SMEM, SMEM, VMEM, VMEM, VMEM, VMEM],
        out_specs=(VMEM, VMEM, VMEM),
        scratch_shapes=[
            pltpu.SMEM((SPANS,), jnp.int32),
            pltpu.VMEM((QROWS, D), BF16),
            pltpu.VMEM((QROWS, D), BF16),
            pltpu.VMEM((D, QROWS), BF16),
            pltpu.VMEM((D, QROWS), BF16),
            pltpu.VMEM((MAX_TILES, TILE, QROWS), BF16),
            pltpu.VMEM((MAX_TILES, 1, QROWS), F32),
            pltpu.VMEM((D, QROWS), F32),
        ],
        compiler_params=pltpu.CompilerParams(vmem_limit_bytes=LIMIT),
        name="attention",
    )(seq, order, seg, q, g, kv)


FAR_FIRST = (4, 3, -3, 2, -2, 1, -1, 0)
UPWARD = (4, -3, 2, -1)


def scatter_kernel(
    part_ref, dk_ref, dv_ref, mine, theirs, landed, load_sem, send_sem, recv_sem, mate_send, mate_recv
):
    me = Place()
    y, z = me.y, me.z
    mate = me.device(core=1 - me.core)

    @pl.when(me.core == 0)
    def _():
        for s in FAR_FIRST:
            pz = me.dz(s)
            pltpu.make_async_copy(
                part_ref.at[:, pz[1], pz[2], 0],
                mine.at[:, pz[1], pz[2]], load_sem.at[pz[0]],
            ).start()

    @pl.when(me.core == 1)
    def _():
        for s in (2, 1, -1, 0):
            py = me.dy(s)
            pltpu.make_async_copy(
                part_ref.at[py, :, :, 1], mine.at[py], load_sem.at[py]
            ).start()

    me.greet(
        [mate]
        + [me.device(y=me.dy(s)) for s in (1, -1, 2)]
        + [me.device(z=me.dz(s)) for s in (1, -1)]
    )
    up_z, down_z = me.device(z=me.dz(1)), me.device(z=me.dz(-1))
    up_y, down_y = me.device(y=me.dy(1)), me.device(y=me.dy(-1))

    def write(total):
        dk_ref[...] = (total[:, :D] * SCALE).astype(BF16)
        dv_ref[...] = total[:, D:].astype(BF16)

    def terms(py, pz, slots):
        at = (py, pz[1], pz[2])
        total = mine[at].astype(F32) + theirs[at].astype(F32)
        for slot in slots:
            arrived(landed.at[slot], mate_send.at[0], recv_sem.at[slot], mate)
            total = total + landed[slot].astype(F32)
        return at, total

    def pass_on(sends, py, pz, slots, slot, device):
        at, total = terms(py, pz, slots)
        mine[at] = total.astype(BF16)
        sends(mine.at[at], landed.at[slot], recv_sem.at[slot], device)

    @pl.when(me.core == 0)
    def _():
        sends = Sends(send_sem)
        mate_sends = Sends(mate_send)
        for s in (2, 1, -1, 0):
            py = me.dy(s)
            mate_sends(part_ref.at[py, :, :, 1], theirs.at[py], mate_recv.at[py], mate)

        def ready(s):
            pz = me.dz(s)
            at = (slice(None), pz[1], pz[2])
            pltpu.make_async_copy(part_ref.at[at + (0,)], mine.at[at], load_sem.at[pz[0]]).wait()
            arrived(theirs.at[at], mate_send.at[0], mate_recv.at[pz[0]], mate)

        order = (0, 1, -1, 2)
        up_slot = lambda s, i: (s - 1) * 4 + order.index(i)
        down_slot = lambda s, i: 16 + (s - 1) * 4 + order.index(i)
        ready(4)
        for i in (0, -1, 1, 2):
            if i in (0, 1):
                pass_on(sends, me.dy(i), me.dz(4), (), up_slot(4, i), up_z)
            else:
                pass_on(sends, me.dy(i), me.dz(4), (), down_slot(4, i), down_z)
        for s in (3, 2, 1):
            ready(s)
            ready(-s)
            for i in order:
                got = (up_slot(s + 1, i),) if s < 3 or i in (0, 1) else ()
                pass_on(sends, me.dy(i), me.dz(s), got, up_slot(s, i), up_z)
                got = (down_slot(s + 1, i),) if s < 3 or i in (-1, 2) else ()
                pass_on(sends, me.dy(i), me.dz(-s), got, down_slot(s, i), down_z)
        ready(0)
        for i in (1, -1, 2):
            pass_on(
                sends, me.dy(i), z, (up_slot(1, i), down_slot(1, i)),
                32 + order.index(i), me.device(y=me.dy(i)),
            )
        _, total = terms(y, z, (up_slot(1, 0), down_slot(1, 0), 33, 34, 35))
        write(total)
        mate_sends.wait()
        sends.wait()

    @pl.when(me.core == 1)
    def _():
        sends = Sends(send_sem)
        mate_sends = Sends(mate_send)
        for s in FAR_FIRST:
            pz = me.dz(s)
            at = (slice(None), pz[1], pz[2])
            mate_sends(part_ref.at[at + (0,)], theirs.at[at], mate_recv.at[pz[0]], mate)

        def ready(s):
            py = me.dy(s)
            pltpu.make_async_copy(part_ref.at[py, :, :, 1], mine.at[py], load_sem.at[py]).wait()
            arrived(theirs.at[py], mate_send.at[0], mate_recv.at[py], mate)

        index = FAR_FIRST.index
        ready(2)
        for s in FAR_FIRST:
            if s in UPWARD:
                pass_on(sends, me.dy(2), me.dz(s), (), index(s), up_y)
            else:
                pass_on(sends, me.dy(2), me.dz(s), (), index(s), down_y)
        ready(1)
        ready(-1)
        for s in FAR_FIRST:
            got = (index(s),)
            pass_on(sends, me.dy(1), me.dz(s), got if s in UPWARD else (), 8 + index(s), up_y)
            pass_on(sends, me.dy(-1), me.dz(s), () if s in UPWARD else got, 16 + index(s), down_y)
        ready(0)
        for s in FAR_FIRST:
            got = (8 + index(s), 16 + index(s))
            if s > 0:
                got += (24 + s + 1,) if s < 4 else ()
                pass_on(sends, y, me.dz(s), got, 24 + s, up_z)
            elif s < 0:
                got += (32 - s + 1,) if s > -3 else ()
                pass_on(sends, y, me.dz(s), got, 32 - s, down_z)
            else:
                _, total = terms(y, z, got + (25, 33))
                write(total)
        mate_sends.wait()
        sends.wait()


def scatter(part):
    return pl.pallas_call(
        scatter_kernel,
        out_shape=(
            jax.ShapeDtypeStruct((ROWS, D), BF16),
            jax.ShapeDtypeStruct((ROWS, D), BF16),
        ),
        in_specs=[ANY],
        out_specs=(VMEM, VMEM),
        scratch_shapes=[
            pltpu.VMEM((4, 2, 4, ROWS, 2 * D), BF16),
            pltpu.VMEM((4, 2, 4, ROWS, 2 * D), BF16),
            pltpu.VMEM((36, ROWS, 2 * D), BF16),
            pltpu.SemaphoreType.DMA((8,)),
            pltpu.SemaphoreType.DMA((40,)),
            pltpu.SemaphoreType.DMA((36,)),
            pltpu.SemaphoreType.DMA((8,)),
            pltpu.SemaphoreType.DMA((8,)),
        ],
        compiler_params=pltpu.CompilerParams(
            collective_id=1, has_side_effects=True, vmem_limit_bytes=LIMIT
        ),
        name="scatter",
    )(part)


def shards(
    query_matrix, key_matrix, value_matrix, segment_ids, block_order, out_weight, d_attended
):
    seq = lax.axis_index(("inner", "outer")).astype(jnp.int32).reshape(1)
    pieces, g = gather(key_matrix, value_matrix, d_attended, out_weight)
    attended, d_queries, terms = attention(
        seq, block_order, segment_ids.reshape(64, 128), query_matrix, g,
        pieces.reshape(TOKENS, 2 * D),
    )
    key_gradient, value_gradient = scatter(terms.reshape(PIECES))
    return (attended, d_queries, key_gradient, value_gradient)


def solution(mesh):
    return jax.shard_map(
        shards,
        mesh=mesh,
        in_specs=(
            P(("inner", "outer"), "tensor"),
            P(("inner", "outer"), "tensor"),
            P(("inner", "outer"), "tensor"),
            P(),
            P(),
            P("tensor", None),
            P(("inner", "outer", "tensor"), None),
        ),
        out_specs=(
            P(("inner", "outer"), "tensor"),
            P(("inner", "outer"), "tensor"),
            P(("inner", "outer"), "tensor"),
            P(("inner", "outer"), "tensor"),
        ),
        check_vma=False,
    )
```

```python
import functools
import math

import jax
import jax.numpy as jnp
from jax import lax
from jax.experimental import pallas as pl
from jax.experimental.pallas import tpu as pltpu
from jax.sharding import PartitionSpec as P

D = 128
HEADS = 8
ROWS = 128
SPAN = 64
SPANS = 128
TOKENS = 8192
QROWS = SPAN * HEADS
UNIT = 8
SIZES = (4, 2, 1)
CHUNK = 128
PER_SUM = 8
LOADS = 8
MOST_KEYS = (65 + UNIT - 1) // UNIT * UNIT * SPAN
SCALE = 1.0 / math.sqrt(D)
EXP2_SCALE = SCALE * math.log2(math.e)
F32 = jnp.float32
BF16 = jnp.bfloat16
MESH = pl.DeviceIdType.MESH
VMEM = pl.BlockSpec(memory_space=pltpu.VMEM)
SMEM = pl.BlockSpec(memory_space=pltpu.SMEM)
ANY = pl.BlockSpec(memory_space=pl.ANY)
LIMIT = 56 * 1024 * 1024
PIECES = (4, 2, 4, 2, ROWS, 2 * D)


class Place:
    def __init__(self):
        inner, outer = lax.axis_index("inner"), lax.axis_index("outer")
        self.x = lax.axis_index("tensor")
        self.y = lax.div(inner, 2)
        self.core = lax.rem(outer, 2)
        z = lax.div(outer, 2) * 2 + lax.rem(inner, 2)
        self.ys = [lax.rem(self.y + s, 4) for s in range(4)]
        self.xs = [lax.rem(self.x + s, 4) for s in range(4)]
        zs = [lax.rem(z + s, 8) for s in range(8)]
        self.zs = [(at, lax.rem(at, 2), lax.div(at, 2)) for at in zs]
        self.z = self.zs[0]

    def dy(self, step):
        return self.ys[step % 4]

    def dz(self, step):
        return self.zs[step % 8]

    def dx(self, step):
        return self.xs[step % 4]

    def device(self, y=None, z=None, core=None, x=None):
        y = self.y if y is None else y
        z = self.z if z is None else z
        core = self.core if core is None else core
        x = self.x if x is None else x
        return (y * 2 + z[1], z[2] * 2 + core, x)

    def greet(self, devices):
        barrier = pltpu.get_barrier_semaphore()
        for device in devices:
            pl.semaphore_signal(barrier, inc=1, device_id=device, device_id_type=MESH)
        pl.semaphore_wait(barrier, len(devices))


class Sends:
    def __init__(self, sems):
        self.sems, self.copies = sems, []

    def __call__(self, src, dst, recv_sem, device):
        copy = pltpu.make_async_remote_copy(
            src_ref=src, dst_ref=dst, send_sem=self.sems.at[len(self.copies)],
            recv_sem=recv_sem, device_id=device, device_id_type=MESH,
        )
        copy.start()
        self.copies.append(copy)

    def wait(self):
        for copy in self.copies:
            copy.wait_send()
        self.copies = []


def arrived(ref, send_sem, recv_sem, device):
    pltpu.make_async_remote_copy(
        src_ref=ref, dst_ref=ref, send_sem=send_sem, recv_sem=recv_sem,
        device_id=device, device_id_type=MESH,
    ).wait_recv()


def piece(ref, y, z, *core):
    return ref.at[(y, z[1], z[2]) + core]


def gather_kernel(
    k_ref, v_ref, da_ref, w_ref, kv_ref, g_ref,
    own, da_all, w_all, local_sem, send_sem, recv_sem, mate_send, mate_recv, x_send, x_recv,
):
    me = Place()
    y, z, x = me.y, me.z, me.x
    w_copy = pltpu.make_async_copy(w_ref, w_all, local_sem.at[0])
    w_copy.start()
    own[:, :D] = k_ref[...]
    own[:, D:] = v_ref[...]
    own_copy = pltpu.make_async_copy(own, piece(kv_ref, y, z, me.core), local_sem.at[1])
    own_copy.start()
    da_all[x] = da_ref[...]
    mate = me.device(core=1 - me.core)
    me.greet(
        [mate]
        + [me.device(y=me.dy(s)) for s in (1, -1, 2)]
        + [me.device(z=me.dz(s)) for s in (1, -1, 2, -2)]
        + [me.device(x=me.dx(s)) for s in (1, -1)]
    )
    up_x, down_x = me.device(x=me.dx(1)), me.device(x=me.dx(-1))
    half = da_ref.shape[1] // 2
    x_sends = Sends(x_send)

    def x_start():
        x_sends(da_ref, da_all.at[x], x_recv.at[0], up_x)
        x_sends(da_ref, da_all.at[x], x_recv.at[1], down_x)

    def x_middle():
        low, high = me.dx(-1), me.dx(1)
        arrived(da_all.at[low], x_send.at[0], x_recv.at[0], mate)
        part = da_all.at[low, :, pl.ds(0, half)]
        x_sends(part, part, x_recv.at[2], up_x)
        arrived(da_all.at[high], x_send.at[0], x_recv.at[1], mate)
        part = da_all.at[high, :, pl.ds(half, half)]
        x_sends(part, part, x_recv.at[3], down_x)

    def x_end():
        far = me.dx(2)
        arrived(da_all.at[far, :, pl.ds(0, half)], x_send.at[0], x_recv.at[2], mate)
        arrived(da_all.at[far, :, pl.ds(half, half)], x_send.at[0], x_recv.at[3], mate)
        w_copy.wait()

    def product(at):
        width = 256
        rows = da_all[...].reshape(ROWS, da_ref.shape[1])
        g_ref[:, at * width:(at + 1) * width] = lax.dot_general(
            rows, w_all[at * width:(at + 1) * width, :], (((1,), (1,)), ((), ())),
            preferred_element_type=F32,
        ).astype(BF16)

    def to_mate(src, dst):
        pltpu.make_async_remote_copy(
            src_ref=src, dst_ref=dst, send_sem=mate_send, recv_sem=mate_recv,
            device_id=mate, device_id_type=MESH,
        ).start()

    def finish(core, sends):
        theirs = kv_ref.at[:, :, :, 1 - core]
        ours = kv_ref.at[:, :, :, core]
        arrived(theirs, mate_send, mate_recv, mate)
        pltpu.make_async_remote_copy(
            src_ref=ours, dst_ref=ours, send_sem=mate_send, recv_sem=mate_recv,
            device_id=mate, device_id_type=MESH,
        ).wait_send()
        sends.wait()
        x_sends.wait()

    up_z, down_z = me.device(z=me.dz(1)), me.device(z=me.dz(-1))
    up_2z, down_2z = me.device(z=me.dz(2)), me.device(z=me.dz(-2))
    up_y, down_y = me.device(y=me.dy(1)), me.device(y=me.dy(-1))

    def fetch(core, sends, step_y, step_z, devices, wait=True):
        py, pz = me.dy(step_y), me.dz(step_z)
        dst = piece(kv_ref, py, pz, core)
        sem = recv_sem.at[py * 8 + pz[0]]
        src = dst if wait else own
        if wait:
            arrived(dst, mate_send, sem, mate)
        for device in devices:
            sends(src, dst, sem, device)
        to_mate(src, dst)

    @pl.when(me.core == 0)
    def _():
        sends = Sends(send_sem)
        fetch(0, sends, 0, 0, [up_y, down_y, me.device(y=me.dy(2)), up_z, down_z], wait=False)
        x_start()
        for i in (1, -1, 2):
            fetch(0, sends, i, 0, [up_z, down_z])
        for i in (0, 1, -1, 2):
            fetch(0, sends, i, -1, [up_z])
            fetch(0, sends, i, 1, [down_z])
        x_middle()
        for i in (0, 1, -1, 2):
            fetch(0, sends, i, -2, [up_2z, up_z] if i in (0, 1) else [up_z])
            fetch(0, sends, i, 2, [down_2z, down_z] if i in (-1, 2) else [down_z])
        x_end()
        for at, i in enumerate((0, 1, -1, 2)):
            product(at)
            fetch(0, sends, i, -3, [])
            fetch(0, sends, i, 3, [])
        for i in (0, -1, 1, 2):
            fetch(0, sends, i, 4, [])
        finish(0, sends)

    @pl.when(me.core == 1)
    def _():
        sends = Sends(send_sem)
        fetch(1, sends, 0, 0, [up_z, down_z, up_2z, down_2z, up_y, down_y], wait=False)
        x_start()

        def across(s):
            fetch(1, sends, -1, s, [up_y] if s <= 0 else [])
            fetch(1, sends, 1, s, [down_y] if s > 0 else [])

        fetch(1, sends, 0, -1, [up_y, down_y])
        fetch(1, sends, 0, 1, [up_y, down_y])
        across(0)
        fetch(1, sends, 0, -2, [up_2z, up_z, up_y, down_y])
        fetch(1, sends, 0, 2, [down_z, up_y, down_y])
        across(-1)
        across(1)
        fetch(1, sends, 0, -3, [up_y, down_y])
        fetch(1, sends, 0, 3, [up_y, down_y])
        across(-2)
        across(2)
        fetch(1, sends, 0, 4, [up_y, down_y])
        x_middle()
        across(-3)
        across(3)
        across(4)
        x_end()
        for at in range(4):
            product(at)
            for s in ((0, -1), (1, -2), (2, -3), (3, 4))[at]:
                fetch(1, sends, 2, s, [])
        finish(1, sends)

    own_copy.wait()


def gather(k, v, da, w):
    return pl.pallas_call(
        gather_kernel,
        out_shape=(
            jax.ShapeDtypeStruct(PIECES, BF16),
            jax.ShapeDtypeStruct((ROWS, w.shape[0]), BF16),
        ),
        in_specs=[VMEM, VMEM, VMEM, ANY],
        out_specs=(ANY, VMEM),
        scratch_shapes=[
            pltpu.VMEM((ROWS, 2 * D), BF16),
            pltpu.VMEM((4,) + da.shape, BF16),
            pltpu.VMEM(w.shape, BF16),
            pltpu.SemaphoreType.DMA((2,)),
            pltpu.SemaphoreType.DMA((48,)),
            pltpu.SemaphoreType.DMA((32,)),
            pltpu.SemaphoreType.DMA,
            pltpu.SemaphoreType.DMA,
            pltpu.SemaphoreType.DMA((4,)),
            pltpu.SemaphoreType.DMA((4,)),
        ],
        compiler_params=pltpu.CompilerParams(
            collective_id=0, has_side_effects=True, vmem_limit_bytes=LIMIT
        ),
        name="gather",
    )(k, v, da, w)


def attention_kernel(
    seq_ref, order_ref, seg_ref, q_ref, g_ref, kv_ref, o_ref, dq_ref, dkv_ref,
    kv, load_sem, stored, qs, gs, q_t, g_t, scores, weights, d_scores, acc,
):
    chunk = TOKENS // LOADS
    loads = [
        pltpu.make_async_copy(
            kv_ref.at[pl.ds(c * chunk, chunk)], kv.at[pl.ds(c * chunk, chunk)], load_sem.at[c]
        )
        for c in range(LOADS)
    ]
    for copy in loads:
        copy.start()
    seq = seq_ref[0]
    for r in range(SPANS):
        stored[order_ref[r]] = r
    seg = seg_ref[...]
    starts = [jnp.sum((seg < d).astype(jnp.int32)) for d in range(1, 8)]
    dkv_ref[...] = jnp.zeros_like(dkv_ref)
    key_iota = lax.broadcasted_iota(jnp.int32, (CHUNK, QROWS), 0)
    lane = lax.broadcasted_iota(jnp.int32, (1, QROWS), 1)

    def begin(position):
        first = jnp.zeros_like(position)
        for start in starts:
            first = jnp.maximum(first, jnp.where(start <= position, start, 0))
        return first

    for copy in loads:
        copy.wait()

    def one_span(half, _):
        row = pl.multiple_of(half * SPAN, SPAN)
        span = order_ref[seq * 2 + half]
        position = span * SPAN + lax.rem(lane, SPAN)
        first = begin(position)
        span_0 = lax.div(begin(span * SPAN), SPAN)
        units = lax.div(span - span_0 + UNIT, UNIT)
        for h in range(HEADS):
            qs[h * SPAN:(h + 1) * SPAN, :] = q_ref[pl.ds(row, SPAN), h * D:(h + 1) * D]
            gs[h * SPAN:(h + 1) * SPAN, :] = g_ref[pl.ds(row, SPAN), h * D:(h + 1) * D]
        q_t[...] = qs[...].T
        g_t[...] = gs[...].T

        def tiles(step, carried):
            done = 0
            for size in SIZES:
                count = lax.div(units - done, size)
                carried = lax.fori_loop(
                    0, count,
                    lambda i, c, size=size, done=done: step(
                        (done + i * size) * UNIT, size * UNIT, c
                    ),
                    carried,
                )
                done = done + count * size
            return carried

        def rows_of(at, count):
            return [
                pl.multiple_of(stored[jnp.minimum(span_0 + at + b, SPANS - 1)] * SPAN, SPAN)
                for b in range(count)
            ]

        def load(rows, column):
            return jnp.concatenate(
                [kv[pl.ds(r, SPAN), column * D:(column + 1) * D] for r in rows], axis=0
            )

        def keys(at, offset, size):
            return pl.ds(pl.multiple_of(at * SPAN, SPAN) + offset, size)

        per = CHUNK // SPAN

        def score(at, count, best):
            rows = rows_of(at, count)
            base = (span_0 + at) * SPAN
            low, high = first - base, position - base
            for c in range(count // per):
                raw = jnp.dot(
                    load(rows[c * per:(c + 1) * per], 0), q_t[...], preferred_element_type=F32
                )
                place = key_iota + c * CHUNK
                raw = jnp.where((place >= low) & (place <= high), raw, -1e30)
                scores[keys(at, c * CHUNK, CHUNK), :] = raw
                best = jnp.maximum(best, jnp.max(raw.reshape(CHUNK // 8, 8, QROWS), axis=0))
            return best

        best = tiles(score, jnp.full((8, QROWS), -1e30, F32))
        top = jnp.max(best, axis=0, keepdims=True) * EXP2_SCALE
        acc[...] = jnp.zeros_like(acc)

        def forward(at, count, total):
            for c in range(count // per):
                part = keys(at, c * CHUNK, CHUNK)
                exponent = jnp.exp2(scores[part, :] * EXP2_SCALE - top)
                weights[part, :] = exponent.astype(BF16)
                total = total + jnp.sum(exponent.reshape(CHUNK // 8, 8, QROWS), axis=0)
            acc[...] += lax.dot_general(
                load(rows_of(at, count), 1), weights[keys(at, 0, count * SPAN), :],
                (((0,), (0,)), ((), ())), preferred_element_type=F32,
            )
            return total

        total = tiles(forward, jnp.zeros((8, QROWS), F32))
        inverse = 1.0 / jnp.sum(total, axis=0, keepdims=True)
        attended_t = (acc[...] * inverse).astype(BF16)
        attended = attended_t.T
        for h in range(HEADS):
            o_ref[pl.ds(row, SPAN), h * D:(h + 1) * D] = attended[h * SPAN:(h + 1) * SPAN, :]
        shrunk = (g_t[...].astype(F32) * inverse).astype(BF16)
        g_t[...] = shrunk
        gs[...] = shrunk.T
        delta = jnp.sum(
            attended_t.astype(F32) * shrunk.astype(F32), axis=0, keepdims=True
        )
        acc[...] = jnp.zeros_like(acc)

        def backward(at, count, carried):
            rows = rows_of(at, count)
            for c in range(count // per):
                d_prob = jnp.dot(
                    load(rows[c * per:(c + 1) * per], 1), g_t[...], preferred_element_type=F32
                )
                weight = weights[keys(at, c * CHUNK, CHUNK), :].astype(F32)
                d_scores[c * CHUNK:(c + 1) * CHUNK, :] = (weight * (d_prob - delta)).astype(BF16)
            acc[...] += lax.dot_general(
                load(rows, 0), d_scores[:count * SPAN, :], (((0,), (0,)), ((), ())),
                preferred_element_type=F32,
            )
            for c in range(count // PER_SUM):
                part = slice(c * PER_SUM * SPAN, (c + 1) * PER_SUM * SPAN)
                dk = jnp.dot(d_scores[part, :], qs[...], preferred_element_type=F32)
                dv = jnp.dot(
                    weights[keys(at, c * PER_SUM * SPAN, PER_SUM * SPAN), :], gs[...],
                    preferred_element_type=F32,
                )
                for b, r in enumerate(rows[c * PER_SUM:(c + 1) * PER_SUM]):
                    for column, terms in enumerate((dk, dv)):
                        place = (pl.ds(r, SPAN), slice(column * D, (column + 1) * D))
                        dkv_ref[place] = (
                            dkv_ref[place].astype(F32) + terms[b * SPAN:(b + 1) * SPAN, :]
                        ).astype(BF16)
            return carried

        tiles(backward, 0)
        dq = (acc[...] * SCALE).astype(BF16).T
        for h in range(HEADS):
            dq_ref[pl.ds(row, SPAN), h * D:(h + 1) * D] = dq[h * SPAN:(h + 1) * SPAN, :]
        return 0

    lax.fori_loop(0, 2, one_span, 0)


def attention(seq, order, seg, q, g, kv):
    return pl.pallas_call(
        attention_kernel,
        out_shape=(
            jax.ShapeDtypeStruct(q.shape, BF16),
            jax.ShapeDtypeStruct(q.shape, BF16),
            jax.ShapeDtypeStruct(kv.shape, BF16),
        ),
        in_specs=[SMEM, SMEM, VMEM, VMEM, VMEM, ANY],
        out_specs=(VMEM, VMEM, VMEM),
        scratch_shapes=[
            pltpu.VMEM(kv.shape, BF16),
            pltpu.SemaphoreType.DMA((LOADS,)),
            pltpu.SMEM((SPANS,), jnp.int32),
            pltpu.VMEM((QROWS, D), BF16),
            pltpu.VMEM((QROWS, D), BF16),
            pltpu.VMEM((D, QROWS), BF16),
            pltpu.VMEM((D, QROWS), BF16),
            pltpu.VMEM((MOST_KEYS, QROWS), F32),
            pltpu.VMEM((MOST_KEYS, QROWS), BF16),
            pltpu.VMEM((max(SIZES) * UNIT * SPAN, QROWS), BF16),
            pltpu.VMEM((D, QROWS), F32),
        ],
        compiler_params=pltpu.CompilerParams(vmem_limit_bytes=LIMIT),
        name="attention",
    )(seq, order, seg, q, g, kv)


FAR_FIRST = (4, 3, -3, 2, -2, 1, -1, 0)
UPWARD = (4, -3, 2, -1)


def scatter_kernel(
    part_ref, sum_ref, mine, theirs, landed, load_sem, send_sem, recv_sem, mate_send, mate_recv
):
    me = Place()
    y, z = me.y, me.z
    mate = me.device(core=1 - me.core)

    def of_z(s):
        return (slice(None),) + me.dz(s)[1:]

    def load_z(s):
        return pltpu.make_async_copy(
            part_ref.at[of_z(s) + (0,)], mine.at[of_z(s)], load_sem.at[me.dz(s)[0]]
        )

    def load_y(s):
        py = me.dy(s)
        return pltpu.make_async_copy(part_ref.at[py, :, :, 1], mine.at[py], load_sem.at[py])

    @pl.when(me.core == 0)
    def _():
        for s in FAR_FIRST:
            load_z(s).start()

    @pl.when(me.core == 1)
    def _():
        for s in (2, 1, -1, 0):
            load_y(s).start()

    me.greet(
        [mate]
        + [me.device(y=me.dy(s)) for s in (1, -1, 2)]
        + [me.device(z=me.dz(s)) for s in (1, -1, 2, -2)]
    )
    up_z, down_z = me.device(z=me.dz(1)), me.device(z=me.dz(-1))
    up_2z, down_2z = me.device(z=me.dz(2)), me.device(z=me.dz(-2))
    up_y, down_y = me.device(y=me.dy(1)), me.device(y=me.dy(-1))
    index = FAR_FIRST.index

    def terms(py, pz, slots):
        at = (py,) + pz[1:]
        total = mine[at].astype(F32) + theirs[at].astype(F32)
        for slot in slots:
            arrived(landed.at[slot], mate_send.at[0], recv_sem.at[slot], mate)
            total = total + landed[slot].astype(F32)
        return at, total

    def pass_on(sends, py, pz, slots, slot, device):
        at, total = terms(py, pz, slots)
        mine[at] = total.astype(BF16)
        sends(mine.at[at], landed.at[slot], recv_sem.at[slot], device)

    @pl.when(me.core == 0)
    def _():
        sends = Sends(send_sem)
        mate_sends = Sends(mate_send)
        for s in FAR_FIRST:
            at = (me.dy(2),) + me.dz(s)[1:]
            mate_sends(
                part_ref.at[at + (1,)], theirs.at[at], mate_recv.at[4 + index(s)], mate
            )
        for s in (1, -1, 0):
            py = me.dy(s)
            mate_sends(part_ref.at[py, :, :, 1], theirs.at[py], mate_recv.at[py], mate)

        def ready(s):
            load_z(s).wait()
            arrived(theirs.at[of_z(s)], mate_send.at[0], mate_recv.at[me.dz(s)[0]], mate)

        order = (0, 1, -1, 2)
        up_slot = lambda s, i: (s - 1) * 4 + order.index(i)
        down_slot = lambda s, i: 16 + (s - 1) * 4 + order.index(i)
        ready(4)
        for i in (0, -1, 1, 2):
            if i in (0, 1):
                pass_on(sends, me.dy(i), me.dz(4), (), up_slot(4, i), up_2z)
            else:
                pass_on(sends, me.dy(i), me.dz(4), (), down_slot(4, i), down_2z)
        for s in (3, 2, 1):
            ready(s)
            ready(-s)
            for i in order:
                got = (up_slot(s + 1, i),) if s < 3 else ()
                got += (up_slot(4, i),) if s == 2 and i in (0, 1) else ()
                pass_on(sends, me.dy(i), me.dz(s), got, up_slot(s, i), up_z)
                got = (down_slot(s + 1, i),) if s < 3 else ()
                got += (down_slot(4, i),) if s == 2 and i in (-1, 2) else ()
                pass_on(sends, me.dy(i), me.dz(-s), got, down_slot(s, i), down_z)
        ready(0)
        for i in (1, -1, 2):
            pass_on(
                sends, me.dy(i), z, (up_slot(1, i), down_slot(1, i)),
                32 + order.index(i), me.device(y=me.dy(i)),
            )
        _, total = terms(y, z, (up_slot(1, 0), down_slot(1, 0), 33, 34, 35))
        sum_ref[...] = total
        mate_sends.wait()
        sends.wait()

    @pl.when(me.core == 1)
    def _():
        sends = Sends(send_sem)
        mate_sends = Sends(mate_send)
        for s in FAR_FIRST:
            at = of_z(s)
            mate_sends(part_ref.at[at + (0,)], theirs.at[at], mate_recv.at[me.dz(s)[0]], mate)

        def ready(s):
            py = me.dy(s)
            load_y(s).wait()
            arrived(theirs.at[py], mate_send.at[0], mate_recv.at[py], mate)

        load_y(2).wait()
        for s in FAR_FIRST:
            at = (me.dy(2),) + me.dz(s)[1:]
            arrived(theirs.at[at], mate_send.at[0], mate_recv.at[4 + index(s)], mate)
            if s in UPWARD:
                pass_on(sends, me.dy(2), me.dz(s), (), index(s), up_y)
            else:
                pass_on(sends, me.dy(2), me.dz(s), (), index(s), down_y)
        ready(1)
        ready(-1)
        for s in FAR_FIRST:
            got = (index(s),)
            pass_on(sends, me.dy(1), me.dz(s), got if s in UPWARD else (), 8 + index(s), up_y)
            pass_on(sends, me.dy(-1), me.dz(s), () if s in UPWARD else got, 16 + index(s), down_y)
        ready(0)
        routes = {
            4: ((), up_2z), 3: ((), up_z), -3: ((), down_z), 2: ((3, 4), up_2z),
            -2: ((-3,), down_2z), 1: ((), up_z), -1: ((), down_z),
        }
        for s in FAR_FIRST[:-1]:
            extra, device = routes[s]
            got = (8 + index(s), 16 + index(s)) + tuple(24 + index(e) for e in extra)
            pass_on(sends, y, me.dz(s), got, 24 + index(s), device)
        got = (15, 23) + tuple(24 + index(e) for e in (1, -1, 2, -2))
        _, total = terms(y, z, got)
        sum_ref[...] = total
        mate_sends.wait()
        sends.wait()


def scatter(part):
    return pl.pallas_call(
        scatter_kernel,
        out_shape=jax.ShapeDtypeStruct((ROWS, 2 * D), F32),
        in_specs=[ANY],
        out_specs=VMEM,
        scratch_shapes=[
            pltpu.VMEM((4, 2, 4, ROWS, 2 * D), BF16),
            pltpu.VMEM((4, 2, 4, ROWS, 2 * D), BF16),
            pltpu.VMEM((36, ROWS, 2 * D), BF16),
            pltpu.SemaphoreType.DMA((8,)),
            pltpu.SemaphoreType.DMA((40,)),
            pltpu.SemaphoreType.DMA((36,)),
            pltpu.SemaphoreType.DMA((12,)),
            pltpu.SemaphoreType.DMA((12,)),
        ],
        compiler_params=pltpu.CompilerParams(
            collective_id=1, has_side_effects=True, vmem_limit_bytes=LIMIT
        ),
        name="scatter",
    )(part)


def shards(
    query_matrix, key_matrix, value_matrix, segment_ids, block_order, out_weight, d_attended
):
    seq = lax.axis_index(("inner", "outer")).astype(jnp.int32).reshape(1)
    pieces, g = gather(key_matrix, value_matrix, d_attended, out_weight)
    attended, d_queries, terms = attention(
        seq, block_order, segment_ids.reshape(64, 128), query_matrix, g,
        pieces.reshape(TOKENS, 2 * D),
    )
    sums = scatter(terms.reshape(PIECES))
    key_gradient = (sums[:, :D] * SCALE).astype(BF16)
    value_gradient = sums[:, D:].astype(BF16)
    return (attended, d_queries, key_gradient, value_gradient)


def solution(mesh):
    return jax.shard_map(
        shards,
        mesh=mesh,
        in_specs=(
            P(("inner", "outer"), "tensor"),
            P(("inner", "outer"), "tensor"),
            P(("inner", "outer"), "tensor"),
            P(),
            P(),
            P("tensor", None),
            P(("inner", "outer", "tensor"), None),
        ),
        out_specs=(
            P(("inner", "outer"), "tensor"),
            P(("inner", "outer"), "tensor"),
            P(("inner", "outer"), "tensor"),
            P(("inner", "outer"), "tensor"),
        ),
        check_vma=False,
    )
```

```python
import functools
import math

import jax
import jax.numpy as jnp
from jax import lax
from jax.experimental import pallas as pl
from jax.experimental.pallas import tpu as pltpu
from jax.sharding import PartitionSpec as P

D = 128
HEADS = 8
ROWS = 128
SPAN = 64
SPANS = 128
TOKENS = 8192
QROWS = SPAN * HEADS
UNIT = 8
SIZES = (4, 2, 1)
CHUNK = 128
PER_SUM = 8
MOST_KEYS = (65 + UNIT - 1) // UNIT * UNIT * SPAN
SCALE = 1.0 / math.sqrt(D)
EXP2_SCALE = SCALE * math.log2(math.e)
F32 = jnp.float32
BF16 = jnp.bfloat16
MESH = pl.DeviceIdType.MESH
VMEM = pl.BlockSpec(memory_space=pltpu.VMEM)
SMEM = pl.BlockSpec(memory_space=pltpu.SMEM)
ANY = pl.BlockSpec(memory_space=pl.ANY)
MIB = 1024 * 1024
GATHER_VMEM, ATTENTION_VMEM, SCATTER_VMEM = 54 * MIB, 34 * MIB, 8 * MIB
PIECES = (4, 2, 4, 2, ROWS, 2 * D)


class Place:
    def __init__(self):
        inner, outer = lax.axis_index("inner"), lax.axis_index("outer")
        self.x = lax.axis_index("tensor")
        self.y = lax.div(inner, 2)
        self.core = lax.rem(outer, 2)
        z = lax.div(outer, 2) * 2 + lax.rem(inner, 2)
        self.ys = [lax.rem(self.y + s, 4) for s in range(4)]
        self.xs = [lax.rem(self.x + s, 4) for s in range(4)]
        zs = [lax.rem(z + s, 8) for s in range(8)]
        self.zs = [(at, lax.rem(at, 2), lax.div(at, 2)) for at in zs]
        self.z = self.zs[0]

    def dy(self, step):
        return self.ys[step % 4]

    def dz(self, step):
        return self.zs[step % 8]

    def dx(self, step):
        return self.xs[step % 4]

    def device(self, y=None, z=None, core=None, x=None):
        y = self.y if y is None else y
        z = self.z if z is None else z
        core = self.core if core is None else core
        x = self.x if x is None else x
        return (y * 2 + z[1], z[2] * 2 + core, x)

    def greet(self, devices):
        barrier = pltpu.get_barrier_semaphore()
        for device in devices:
            pl.semaphore_signal(barrier, inc=1, device_id=device, device_id_type=MESH)
        pl.semaphore_wait(barrier, len(devices))


class Sends:
    def __init__(self, sems):
        self.sems, self.copies = sems, []

    def __call__(self, src, dst, recv_sem, device):
        copy = pltpu.make_async_remote_copy(
            src_ref=src, dst_ref=dst, send_sem=self.sems.at[len(self.copies)],
            recv_sem=recv_sem, device_id=device, device_id_type=MESH,
        )
        copy.start()
        self.copies.append(copy)

    def wait(self):
        for copy in self.copies:
            copy.wait_send()
        self.copies = []


def arrived(ref, send_sem, recv_sem, device):
    pltpu.make_async_remote_copy(
        src_ref=ref, dst_ref=ref, send_sem=send_sem, recv_sem=recv_sem,
        device_id=device, device_id_type=MESH,
    ).wait_recv()


def piece(ref, y, z, *core):
    return ref.at[(y, z[1], z[2]) + core]


def gather_kernel(
    k_ref, v_ref, da_ref, w_ref, kv_ref, g_ref,
    own, da_all, w_all, local_sem, send_sem, recv_sem, mate_send, mate_recv, x_send, x_recv,
):
    me = Place()
    y, z, x = me.y, me.z, me.x
    w_copy = pltpu.make_async_copy(w_ref, w_all, local_sem.at[0])
    w_copy.start()
    own[:, :D] = k_ref[...]
    own[:, D:] = v_ref[...]
    own_copy = pltpu.make_async_copy(own, piece(kv_ref, y, z, me.core), local_sem.at[1])
    own_copy.start()
    da_all[x] = da_ref[...]
    mate = me.device(core=1 - me.core)
    me.greet(
        [mate]
        + [me.device(y=me.dy(s)) for s in (1, -1, 2)]
        + [me.device(z=me.dz(s)) for s in (1, -1, 2, -2)]
        + [me.device(x=me.dx(s)) for s in (1, -1)]
    )
    up_x, down_x = me.device(x=me.dx(1)), me.device(x=me.dx(-1))
    half = da_ref.shape[1] // 2
    x_sends = Sends(x_send)

    def x_start():
        x_sends(da_ref, da_all.at[x], x_recv.at[0], up_x)
        x_sends(da_ref, da_all.at[x], x_recv.at[1], down_x)

    def x_middle():
        low, high = me.dx(-1), me.dx(1)
        arrived(da_all.at[low], x_send.at[0], x_recv.at[0], mate)
        part = da_all.at[low, :, pl.ds(0, half)]
        x_sends(part, part, x_recv.at[2], up_x)
        arrived(da_all.at[high], x_send.at[0], x_recv.at[1], mate)
        part = da_all.at[high, :, pl.ds(half, half)]
        x_sends(part, part, x_recv.at[3], down_x)

    def x_end():
        far = me.dx(2)
        arrived(da_all.at[far, :, pl.ds(0, half)], x_send.at[0], x_recv.at[2], mate)
        arrived(da_all.at[far, :, pl.ds(half, half)], x_send.at[0], x_recv.at[3], mate)
        w_copy.wait()

    def product(at):
        width = 256
        rows = da_all[...].reshape(ROWS, da_ref.shape[1])
        g_ref[:, at * width:(at + 1) * width] = lax.dot_general(
            rows, w_all[at * width:(at + 1) * width, :], (((1,), (1,)), ((), ())),
            preferred_element_type=F32,
        ).astype(BF16)

    def to_mate(src, dst):
        pltpu.make_async_remote_copy(
            src_ref=src, dst_ref=dst, send_sem=mate_send, recv_sem=mate_recv,
            device_id=mate, device_id_type=MESH,
        ).start()

    def finish(core, sends):
        theirs = kv_ref.at[:, :, :, 1 - core]
        ours = kv_ref.at[:, :, :, core]
        arrived(theirs, mate_send, mate_recv, mate)
        pltpu.make_async_remote_copy(
            src_ref=ours, dst_ref=ours, send_sem=mate_send, recv_sem=mate_recv,
            device_id=mate, device_id_type=MESH,
        ).wait_send()
        sends.wait()
        x_sends.wait()

    up_z, down_z = me.device(z=me.dz(1)), me.device(z=me.dz(-1))
    up_2z, down_2z = me.device(z=me.dz(2)), me.device(z=me.dz(-2))
    up_y, down_y = me.device(y=me.dy(1)), me.device(y=me.dy(-1))

    def fetch(core, sends, step_y, step_z, devices, wait=True):
        py, pz = me.dy(step_y), me.dz(step_z)
        dst = piece(kv_ref, py, pz, core)
        sem = recv_sem.at[py * 8 + pz[0]]
        src = dst if wait else own
        if wait:
            arrived(dst, mate_send, sem, mate)
        for device in devices:
            sends(src, dst, sem, device)
        to_mate(src, dst)

    @pl.when(me.core == 0)
    def _():
        sends = Sends(send_sem)
        fetch(0, sends, 0, 0, [up_y, down_y, me.device(y=me.dy(2)), up_z, down_z], wait=False)
        x_start()
        for i in (1, -1, 2):
            fetch(0, sends, i, 0, [up_z, down_z])
        for i in (0, 1, -1, 2):
            fetch(0, sends, i, -1, [up_z])
            fetch(0, sends, i, 1, [down_z])
        x_middle()
        for i in (0, 1, -1, 2):
            fetch(0, sends, i, -2, [up_2z, up_z] if i in (0, 1) else [up_z])
            fetch(0, sends, i, 2, [down_2z, down_z] if i in (-1, 2) else [down_z])
        x_end()
        for at, i in enumerate((0, 1, -1, 2)):
            product(at)
            fetch(0, sends, i, -3, [])
            fetch(0, sends, i, 3, [])
        for i in (0, -1, 1, 2):
            fetch(0, sends, i, 4, [])
        finish(0, sends)

    @pl.when(me.core == 1)
    def _():
        sends = Sends(send_sem)
        fetch(1, sends, 0, 0, [up_z, down_z, up_2z, down_2z, up_y, down_y], wait=False)
        x_start()

        def across(s):
            fetch(1, sends, -1, s, [up_y] if s <= 0 else [])
            fetch(1, sends, 1, s, [down_y] if s > 0 else [])

        fetch(1, sends, 0, -1, [up_y, down_y])
        fetch(1, sends, 0, 1, [up_y, down_y])
        across(0)
        fetch(1, sends, 0, -2, [up_2z, up_z, up_y, down_y])
        fetch(1, sends, 0, 2, [down_z, up_y, down_y])
        across(-1)
        across(1)
        fetch(1, sends, 0, -3, [up_y, down_y])
        fetch(1, sends, 0, 3, [up_y, down_y])
        across(-2)
        across(2)
        fetch(1, sends, 0, 4, [up_y, down_y])
        x_middle()
        across(-3)
        across(3)
        across(4)
        x_end()
        for at in range(4):
            product(at)
            for s in ((0, -1), (1, -2), (2, -3), (3, 4))[at]:
                fetch(1, sends, 2, s, [])
        finish(1, sends)

    own_copy.wait()


def gather(k, v, da, w):
    return pl.pallas_call(
        gather_kernel,
        out_shape=(
            pltpu.VMEM(PIECES, BF16),
            pltpu.VMEM((ROWS, w.shape[0]), BF16),
        ),
        in_specs=[VMEM, VMEM, VMEM, ANY],
        out_specs=(ANY, VMEM),
        scratch_shapes=[
            pltpu.VMEM((ROWS, 2 * D), BF16),
            pltpu.VMEM((4,) + da.shape, BF16),
            pltpu.VMEM(w.shape, BF16),
            pltpu.SemaphoreType.DMA((2,)),
            pltpu.SemaphoreType.DMA((48,)),
            pltpu.SemaphoreType.DMA((32,)),
            pltpu.SemaphoreType.DMA,
            pltpu.SemaphoreType.DMA,
            pltpu.SemaphoreType.DMA((4,)),
            pltpu.SemaphoreType.DMA((4,)),
        ],
        compiler_params=pltpu.CompilerParams(
            collective_id=0, has_side_effects=True, vmem_limit_bytes=GATHER_VMEM
        ),
        name="gather",
    )(k, v, da, w)


def attention_kernel(
    seq_ref, order_ref, seg_ref, q_ref, g_ref, kv, o_ref, dq_ref, dkv_ref,
    stored, qs, gs, q_t, g_t, scores, weights, d_scores, acc,
):
    seq = seq_ref[0]
    for r in range(SPANS):
        stored[order_ref[r]] = r
    seg = seg_ref[...]
    starts = [jnp.sum((seg < d).astype(jnp.int32)) for d in range(1, 8)]
    dkv_ref[...] = jnp.zeros_like(dkv_ref)
    key_iota = lax.broadcasted_iota(jnp.int32, (CHUNK, QROWS), 0)
    lane = lax.broadcasted_iota(jnp.int32, (1, QROWS), 1)

    def begin(position):
        first = jnp.zeros_like(position)
        for start in starts:
            first = jnp.maximum(first, jnp.where(start <= position, start, 0))
        return first

    def one_span(half, _):
        row = pl.multiple_of(half * SPAN, SPAN)
        span = order_ref[seq * 2 + half]
        position = span * SPAN + lax.rem(lane, SPAN)
        first = begin(position)
        span_0 = lax.div(begin(span * SPAN), SPAN)
        units = lax.div(span - span_0 + UNIT, UNIT)
        for h in range(HEADS):
            qs[h * SPAN:(h + 1) * SPAN, :] = q_ref[pl.ds(row, SPAN), h * D:(h + 1) * D]
            gs[h * SPAN:(h + 1) * SPAN, :] = g_ref[pl.ds(row, SPAN), h * D:(h + 1) * D]
        q_t[...] = qs[...].T
        g_t[...] = gs[...].T

        def tiles(step, carried):
            done = 0
            for size in SIZES:
                count = lax.div(units - done, size)
                carried = lax.fori_loop(
                    0, count,
                    lambda i, c, size=size, done=done: step(
                        (done + i * size) * UNIT, size * UNIT, c
                    ),
                    carried,
                )
                done = done + count * size
            return carried

        def rows_of(at, count):
            return [
                pl.multiple_of(stored[jnp.minimum(span_0 + at + b, SPANS - 1)] * SPAN, SPAN)
                for b in range(count)
            ]

        def load(rows, column):
            return jnp.concatenate(
                [kv[pl.ds(r, SPAN), column * D:(column + 1) * D] for r in rows], axis=0
            )

        def keys(at, offset, size):
            return pl.ds(pl.multiple_of(at * SPAN, SPAN) + offset, size)

        per = CHUNK // SPAN

        def score(at, count, best):
            rows = rows_of(at, count)
            base = (span_0 + at) * SPAN
            low, high = first - base, position - base
            for c in range(count // per):
                raw = jnp.dot(
                    load(rows[c * per:(c + 1) * per], 0), q_t[...], preferred_element_type=F32
                )
                place = key_iota + c * CHUNK
                raw = jnp.where((place >= low) & (place <= high), raw, -1e30)
                scores[keys(at, c * CHUNK, CHUNK), :] = raw
                best = jnp.maximum(best, jnp.max(raw.reshape(CHUNK // 8, 8, QROWS), axis=0))
            return best

        best = tiles(score, jnp.full((8, QROWS), -1e30, F32))
        top = jnp.max(best, axis=0, keepdims=True) * EXP2_SCALE
        acc[...] = jnp.zeros_like(acc)

        def forward(at, count, total):
            for c in range(count // per):
                part = keys(at, c * CHUNK, CHUNK)
                exponent = jnp.exp2(scores[part, :] * EXP2_SCALE - top)
                weights[part, :] = exponent.astype(BF16)
                total = total + jnp.sum(exponent.reshape(CHUNK // 8, 8, QROWS), axis=0)
            acc[...] += lax.dot_general(
                load(rows_of(at, count), 1), weights[keys(at, 0, count * SPAN), :],
                (((0,), (0,)), ((), ())), preferred_element_type=F32,
            )
            return total

        total = tiles(forward, jnp.zeros((8, QROWS), F32))
        inverse = 1.0 / jnp.sum(total, axis=0, keepdims=True)
        attended_t = (acc[...] * inverse).astype(BF16)
        attended = attended_t.T
        for h in range(HEADS):
            o_ref[pl.ds(row, SPAN), h * D:(h + 1) * D] = attended[h * SPAN:(h + 1) * SPAN, :]
        shrunk = (g_t[...].astype(F32) * inverse).astype(BF16)
        g_t[...] = shrunk
        gs[...] = shrunk.T
        delta = jnp.sum(
            attended_t.astype(F32) * shrunk.astype(F32), axis=0, keepdims=True
        )
        acc[...] = jnp.zeros_like(acc)

        def backward(at, count, carried):
            rows = rows_of(at, count)
            for c in range(count // per):
                d_prob = jnp.dot(
                    load(rows[c * per:(c + 1) * per], 1), g_t[...], preferred_element_type=F32
                )
                weight = weights[keys(at, c * CHUNK, CHUNK), :].astype(F32)
                d_scores[c * CHUNK:(c + 1) * CHUNK, :] = (weight * (d_prob - delta)).astype(BF16)
            acc[...] += lax.dot_general(
                load(rows, 0), d_scores[:count * SPAN, :], (((0,), (0,)), ((), ())),
                preferred_element_type=F32,
            )
            for c in range(count // PER_SUM):
                part = slice(c * PER_SUM * SPAN, (c + 1) * PER_SUM * SPAN)
                dk = jnp.dot(d_scores[part, :], qs[...], preferred_element_type=F32)
                dv = jnp.dot(
                    weights[keys(at, c * PER_SUM * SPAN, PER_SUM * SPAN), :], gs[...],
                    preferred_element_type=F32,
                )
                for b, r in enumerate(rows[c * PER_SUM:(c + 1) * PER_SUM]):
                    for column, terms in enumerate((dk, dv)):
                        place = (pl.ds(r, SPAN), slice(column * D, (column + 1) * D))
                        dkv_ref[place] = (
                            dkv_ref[place].astype(F32) + terms[b * SPAN:(b + 1) * SPAN, :]
                        ).astype(BF16)
            return carried

        tiles(backward, 0)
        dq = (acc[...] * SCALE).astype(BF16).T
        for h in range(HEADS):
            dq_ref[pl.ds(row, SPAN), h * D:(h + 1) * D] = dq[h * SPAN:(h + 1) * SPAN, :]
        return 0

    lax.fori_loop(0, 2, one_span, 0)


def attention(seq, order, seg, q, g, kv):
    return pl.pallas_call(
        attention_kernel,
        out_shape=(
            jax.ShapeDtypeStruct(q.shape, BF16),
            jax.ShapeDtypeStruct(q.shape, BF16),
            jax.ShapeDtypeStruct(kv.shape, BF16),
        ),
        in_specs=[SMEM, SMEM, VMEM, VMEM, VMEM, VMEM],
        out_specs=(VMEM, VMEM, VMEM),
        scratch_shapes=[
            pltpu.SMEM((SPANS,), jnp.int32),
            pltpu.VMEM((QROWS, D), BF16),
            pltpu.VMEM((QROWS, D), BF16),
            pltpu.VMEM((D, QROWS), BF16),
            pltpu.VMEM((D, QROWS), BF16),
            pltpu.VMEM((MOST_KEYS, QROWS), F32),
            pltpu.VMEM((MOST_KEYS, QROWS), BF16),
            pltpu.VMEM((max(SIZES) * UNIT * SPAN, QROWS), BF16),
            pltpu.VMEM((D, QROWS), F32),
        ],
        compiler_params=pltpu.CompilerParams(vmem_limit_bytes=ATTENTION_VMEM),
        name="attention",
    )(seq, order, seg, q, g, kv)


FAR_FIRST = (4, 3, -3, 2, -2, 1, -1, 0)
UPWARD = (4, -3, 2, -1)


def scatter_kernel(
    part_ref, sum_ref, mine, theirs, landed, load_sem, send_sem, recv_sem, mate_send, mate_recv
):
    me = Place()
    y, z = me.y, me.z
    mate = me.device(core=1 - me.core)

    def of_z(s):
        return (slice(None),) + me.dz(s)[1:]

    def load_z(s):
        return pltpu.make_async_copy(
            part_ref.at[of_z(s) + (0,)], mine.at[of_z(s)], load_sem.at[me.dz(s)[0]]
        )

    def load_y(s):
        py = me.dy(s)
        return pltpu.make_async_copy(part_ref.at[py, :, :, 1], mine.at[py], load_sem.at[py])

    @pl.when(me.core == 0)
    def _():
        for s in FAR_FIRST:
            load_z(s).start()

    @pl.when(me.core == 1)
    def _():
        for s in (2, 1, -1, 0):
            load_y(s).start()

    me.greet(
        [mate]
        + [me.device(y=me.dy(s)) for s in (1, -1, 2)]
        + [me.device(z=me.dz(s)) for s in (1, -1, 2, -2)]
    )
    up_z, down_z = me.device(z=me.dz(1)), me.device(z=me.dz(-1))
    up_2z, down_2z = me.device(z=me.dz(2)), me.device(z=me.dz(-2))
    up_y, down_y = me.device(y=me.dy(1)), me.device(y=me.dy(-1))
    index = FAR_FIRST.index

    def terms(py, pz, slots):
        at = (py,) + pz[1:]
        total = mine[at].astype(F32) + theirs[at].astype(F32)
        for slot in slots:
            arrived(landed.at[slot], mate_send.at[0], recv_sem.at[slot], mate)
            total = total + landed[slot].astype(F32)
        return at, total

    def pass_on(sends, py, pz, slots, slot, device):
        at, total = terms(py, pz, slots)
        mine[at] = total.astype(BF16)
        sends(mine.at[at], landed.at[slot], recv_sem.at[slot], device)

    @pl.when(me.core == 0)
    def _():
        sends = Sends(send_sem)
        mate_sends = Sends(mate_send)
        for s in FAR_FIRST:
            at = (me.dy(2),) + me.dz(s)[1:]
            mate_sends(
                part_ref.at[at + (1,)], theirs.at[at], mate_recv.at[4 + index(s)], mate
            )
        for s in (1, -1, 0):
            py = me.dy(s)
            mate_sends(part_ref.at[py, :, :, 1], theirs.at[py], mate_recv.at[py], mate)

        def ready(s):
            load_z(s).wait()
            arrived(theirs.at[of_z(s)], mate_send.at[0], mate_recv.at[me.dz(s)[0]], mate)

        order = (0, 1, -1, 2)
        up_slot = lambda s, i: (s - 1) * 4 + order.index(i)
        down_slot = lambda s, i: 16 + (s - 1) * 4 + order.index(i)
        ready(4)
        for i in (0, -1, 1, 2):
            if i in (0, 1):
                pass_on(sends, me.dy(i), me.dz(4), (), up_slot(4, i), up_2z)
            else:
                pass_on(sends, me.dy(i), me.dz(4), (), down_slot(4, i), down_2z)
        for s in (3, 2, 1):
            ready(s)
            ready(-s)
            for i in order:
                got = (up_slot(s + 1, i),) if s < 3 else ()
                got += (up_slot(4, i),) if s == 2 and i in (0, 1) else ()
                pass_on(sends, me.dy(i), me.dz(s), got, up_slot(s, i), up_z)
                got = (down_slot(s + 1, i),) if s < 3 else ()
                got += (down_slot(4, i),) if s == 2 and i in (-1, 2) else ()
                pass_on(sends, me.dy(i), me.dz(-s), got, down_slot(s, i), down_z)
        ready(0)
        for i in (1, -1, 2):
            pass_on(
                sends, me.dy(i), z, (up_slot(1, i), down_slot(1, i)),
                32 + order.index(i), me.device(y=me.dy(i)),
            )
        _, total = terms(y, z, (up_slot(1, 0), down_slot(1, 0), 33, 34, 35))
        sum_ref[...] = total
        mate_sends.wait()
        sends.wait()

    @pl.when(me.core == 1)
    def _():
        sends = Sends(send_sem)
        mate_sends = Sends(mate_send)
        for s in FAR_FIRST:
            at = of_z(s)
            mate_sends(part_ref.at[at + (0,)], theirs.at[at], mate_recv.at[me.dz(s)[0]], mate)

        def ready(s):
            py = me.dy(s)
            load_y(s).wait()
            arrived(theirs.at[py], mate_send.at[0], mate_recv.at[py], mate)

        load_y(2).wait()
        for s in FAR_FIRST:
            at = (me.dy(2),) + me.dz(s)[1:]
            arrived(theirs.at[at], mate_send.at[0], mate_recv.at[4 + index(s)], mate)
            if s in UPWARD:
                pass_on(sends, me.dy(2), me.dz(s), (), index(s), up_y)
            else:
                pass_on(sends, me.dy(2), me.dz(s), (), index(s), down_y)
        ready(1)
        ready(-1)
        for s in FAR_FIRST:
            got = (index(s),)
            pass_on(sends, me.dy(1), me.dz(s), got if s in UPWARD else (), 8 + index(s), up_y)
            pass_on(sends, me.dy(-1), me.dz(s), () if s in UPWARD else got, 16 + index(s), down_y)
        ready(0)
        routes = {
            4: ((), up_2z), 3: ((), up_z), -3: ((), down_z), 2: ((3, 4), up_2z),
            -2: ((-3,), down_2z), 1: ((), up_z), -1: ((), down_z),
        }
        for s in FAR_FIRST[:-1]:
            extra, device = routes[s]
            got = (8 + index(s), 16 + index(s)) + tuple(24 + index(e) for e in extra)
            pass_on(sends, y, me.dz(s), got, 24 + index(s), device)
        got = (15, 23) + tuple(24 + index(e) for e in (1, -1, 2, -2))
        _, total = terms(y, z, got)
        sum_ref[...] = total
        mate_sends.wait()
        sends.wait()


def scatter(part):
    return pl.pallas_call(
        scatter_kernel,
        out_shape=jax.ShapeDtypeStruct((ROWS, 2 * D), F32),
        in_specs=[ANY],
        out_specs=VMEM,
        scratch_shapes=[
            pltpu.VMEM((4, 2, 4, ROWS, 2 * D), BF16),
            pltpu.VMEM((4, 2, 4, ROWS, 2 * D), BF16),
            pltpu.VMEM((36, ROWS, 2 * D), BF16),
            pltpu.SemaphoreType.DMA((8,)),
            pltpu.SemaphoreType.DMA((40,)),
            pltpu.SemaphoreType.DMA((36,)),
            pltpu.SemaphoreType.DMA((12,)),
            pltpu.SemaphoreType.DMA((12,)),
        ],
        compiler_params=pltpu.CompilerParams(
            collective_id=1, has_side_effects=True, vmem_limit_bytes=SCATTER_VMEM
        ),
        name="scatter",
    )(part)


def finish_kernel(sum_ref, dk_ref, dv_ref):
    dk_ref[...] = (sum_ref[:, :D] * SCALE).astype(BF16)
    dv_ref[...] = sum_ref[:, D:].astype(BF16)


def finish(sums):
    return pl.pallas_call(
        finish_kernel,
        out_shape=(jax.ShapeDtypeStruct((ROWS, D), BF16),) * 2,
        in_specs=[VMEM],
        out_specs=(VMEM, VMEM),
        compiler_params=pltpu.CompilerParams(vmem_limit_bytes=2 * MIB),
        name="finish",
    )(sums)


def shards(
    query_matrix, key_matrix, value_matrix, segment_ids, block_order, out_weight, d_attended
):
    seq = lax.axis_index(("inner", "outer")).astype(jnp.int32).reshape(1)
    pieces, g = gather(key_matrix, value_matrix, d_attended, out_weight)
    attended, d_queries, terms = attention(
        seq, block_order, segment_ids.reshape(64, 128), query_matrix, g,
        pieces.reshape(TOKENS, 2 * D),
    )
    sums = scatter(terms.reshape(PIECES))
    key_gradient, value_gradient = finish(sums)
    return (attended, d_queries, key_gradient, value_gradient)


def solution(mesh):
    return jax.shard_map(
        shards,
        mesh=mesh,
        in_specs=(
            P(("inner", "outer"), "tensor"),
            P(("inner", "outer"), "tensor"),
            P(("inner", "outer"), "tensor"),
            P(),
            P(),
            P("tensor", None),
            P(("inner", "outer", "tensor"), None),
        ),
        out_specs=(
            P(("inner", "outer"), "tensor"),
            P(("inner", "outer"), "tensor"),
            P(("inner", "outer"), "tensor"),
            P(("inner", "outer"), "tensor"),
        ),
        check_vma=False,
    )
```

```python
import functools
import math

import jax
import jax.numpy as jnp
from jax import lax
from jax.experimental import pallas as pl
from jax.experimental.pallas import tpu as pltpu
from jax.sharding import PartitionSpec as P

D = 128
HEADS = 8
ROWS = 128
SPAN = 64
SPANS = 128
TOKENS = 8192
QROWS = SPAN * HEADS
UNIT = 8
SIZES = (4, 2, 1)
CHUNK = 128
PER_MIX, PER_SUM, SLOPE = 8, 8, 512
MOST_KEYS = (65 + UNIT - 1) // UNIT * UNIT * SPAN
SCALE = 1.0 / math.sqrt(D)
EXP2_SCALE = SCALE * math.log2(math.e)
F32 = jnp.float32
BF16 = jnp.bfloat16
MESH = pl.DeviceIdType.MESH
VMEM = pl.BlockSpec(memory_space=pltpu.VMEM)
SMEM = pl.BlockSpec(memory_space=pltpu.SMEM)
ANY = pl.BlockSpec(memory_space=pl.ANY)
MIB = 1024 * 1024
GATHER_VMEM, ATTENTION_VMEM, SCATTER_VMEM = 54 * MIB, 34 * MIB, 8 * MIB
PIECES = (4, 2, 4, 2, ROWS, 2 * D)


class Place:
    def __init__(self):
        inner, outer = lax.axis_index("inner"), lax.axis_index("outer")
        self.x = lax.axis_index("tensor")
        self.y = lax.div(inner, 2)
        self.core = lax.rem(outer, 2)
        z = lax.div(outer, 2) * 2 + lax.rem(inner, 2)
        self.ys = [lax.rem(self.y + s, 4) for s in range(4)]
        self.xs = [lax.rem(self.x + s, 4) for s in range(4)]
        zs = [lax.rem(z + s, 8) for s in range(8)]
        self.zs = [(at, lax.rem(at, 2), lax.div(at, 2)) for at in zs]
        self.z = self.zs[0]

    def dy(self, step):
        return self.ys[step % 4]

    def dz(self, step):
        return self.zs[step % 8]

    def dx(self, step):
        return self.xs[step % 4]

    def device(self, y=None, z=None, core=None, x=None):
        y = self.y if y is None else y
        z = self.z if z is None else z
        core = self.core if core is None else core
        x = self.x if x is None else x
        return (y * 2 + z[1], z[2] * 2 + core, x)

    def greet(self, devices):
        barrier = pltpu.get_barrier_semaphore()
        for device in devices:
            pl.semaphore_signal(barrier, inc=1, device_id=device, device_id_type=MESH)
        pl.semaphore_wait(barrier, len(devices))


class Sends:
    def __init__(self, sems):
        self.sems, self.copies = sems, []

    def __call__(self, src, dst, recv_sem, device):
        copy = pltpu.make_async_remote_copy(
            src_ref=src, dst_ref=dst, send_sem=self.sems.at[len(self.copies)],
            recv_sem=recv_sem, device_id=device, device_id_type=MESH,
        )
        copy.start()
        self.copies.append(copy)

    def wait(self):
        for copy in self.copies:
            copy.wait_send()
        self.copies = []


def arrived(ref, send_sem, recv_sem, device):
    pltpu.make_async_remote_copy(
        src_ref=ref, dst_ref=ref, send_sem=send_sem, recv_sem=recv_sem,
        device_id=device, device_id_type=MESH,
    ).wait_recv()


def piece(ref, y, z, *core):
    return ref.at[(y, z[1], z[2]) + core]


def gather_kernel(
    k_ref, v_ref, da_ref, w_ref, kv_ref, g_ref,
    own, da_all, w_all, local_sem, send_sem, recv_sem, mate_send, mate_recv, x_send, x_recv,
):
    me = Place()
    y, z, x = me.y, me.z, me.x
    w_copy = pltpu.make_async_copy(w_ref, w_all, local_sem.at[0])
    w_copy.start()
    own[:, :D] = k_ref[...]
    own[:, D:] = v_ref[...]
    own_copy = pltpu.make_async_copy(own, piece(kv_ref, y, z, me.core), local_sem.at[1])
    own_copy.start()
    da_all[x] = da_ref[...]
    mate = me.device(core=1 - me.core)
    me.greet(
        [mate]
        + [me.device(y=me.dy(s)) for s in (1, -1, 2)]
        + [me.device(z=me.dz(s)) for s in (1, -1, 2, -2)]
        + [me.device(x=me.dx(s)) for s in (1, -1)]
    )
    up_x, down_x = me.device(x=me.dx(1)), me.device(x=me.dx(-1))
    half = da_ref.shape[1] // 2
    x_sends = Sends(x_send)

    def x_start():
        x_sends(da_ref, da_all.at[x], x_recv.at[0], up_x)
        x_sends(da_ref, da_all.at[x], x_recv.at[1], down_x)

    def x_middle():
        low, high = me.dx(-1), me.dx(1)
        arrived(da_all.at[low], x_send.at[0], x_recv.at[0], mate)
        part = da_all.at[low, :, pl.ds(0, half)]
        x_sends(part, part, x_recv.at[2], up_x)
        arrived(da_all.at[high], x_send.at[0], x_recv.at[1], mate)
        part = da_all.at[high, :, pl.ds(half, half)]
        x_sends(part, part, x_recv.at[3], down_x)

    def x_end():
        far = me.dx(2)
        arrived(da_all.at[far, :, pl.ds(0, half)], x_send.at[0], x_recv.at[2], mate)
        arrived(da_all.at[far, :, pl.ds(half, half)], x_send.at[0], x_recv.at[3], mate)
        w_copy.wait()

    def product(step, _):
        width = 256
        at = pl.ds(pl.multiple_of(step * width, width), width)
        rows = da_all[...].reshape(ROWS, da_ref.shape[1])
        g_ref[:, at] = lax.dot_general(
            rows, w_all[at, :], (((1,), (1,)), ((), ())), preferred_element_type=F32
        ).astype(BF16)
        return 0

    def to_mate(src, dst):
        pltpu.make_async_remote_copy(
            src_ref=src, dst_ref=dst, send_sem=mate_send, recv_sem=mate_recv,
            device_id=mate, device_id_type=MESH,
        ).start()

    up_z, down_z = me.device(z=me.dz(1)), me.device(z=me.dz(-1))
    up_2z, down_2z = me.device(z=me.dz(2)), me.device(z=me.dz(-2))
    up_y, down_y = me.device(y=me.dy(1)), me.device(y=me.dy(-1))

    def fetch(core, sends, step_y, step_z, devices, wait=True):
        py, pz = me.dy(step_y), me.dz(step_z)
        dst = piece(kv_ref, py, pz, core)
        sem = recv_sem.at[py * 8 + pz[0]]
        src = dst if wait else own
        if wait:
            arrived(dst, mate_send, sem, mate)
        for device in devices:
            sends(src, dst, sem, device)
        to_mate(src, dst)

    @pl.when(me.core == 0)
    def _():
        sends = Sends(send_sem)
        fetch(0, sends, 0, 0, [up_y, down_y, me.device(y=me.dy(2)), up_z, down_z], wait=False)
        x_start()
        for i in (1, -1, 2):
            fetch(0, sends, i, 0, [up_z, down_z])
        for i in (0, 1, -1, 2):
            fetch(0, sends, i, -1, [up_z])
            fetch(0, sends, i, 1, [down_z])
        x_middle()
        for i in (0, 1, -1, 2):
            fetch(0, sends, i, -2, [up_2z, up_z] if i in (0, 1) else [up_z])
            fetch(0, sends, i, 2, [down_2z, down_z] if i in (-1, 2) else [down_z])
        for i in (0, 1, -1, 2):
            fetch(0, sends, i, -3, [])
            fetch(0, sends, i, 3, [])
        for i in (0, -1, 1, 2):
            fetch(0, sends, i, 4, [])
        sends.wait()
        x_sends.wait()

    @pl.when(me.core == 1)
    def _():
        sends = Sends(send_sem)
        ys = [up_y, down_y]
        fetch(1, sends, 0, 0, [up_z, down_z, up_2z, down_2z] + ys, wait=False)
        x_start()

        def across(s):
            fetch(1, sends, -1, s, [up_y] if s <= 0 else [])
            fetch(1, sends, 1, s, [down_y] if s > 0 else [])

        fetch(1, sends, 0, -1, ys)
        fetch(1, sends, 0, 1, ys)
        across(0)
        fetch(1, sends, 0, -2, [up_2z, up_z] + ys)
        fetch(1, sends, 0, 2, [down_z] + ys)
        across(-1)
        across(1)
        fetch(1, sends, 0, -3, ys)
        fetch(1, sends, 0, 3, ys)
        across(-2)
        across(2)
        fetch(1, sends, 0, 4, ys)
        x_middle()
        for s in (-3, 3, 4):
            across(s)
        for s in (0, -1, 1, -2, 2, -3, 3, 4):
            fetch(1, sends, 2, s, [])
        sends.wait()
        x_sends.wait()

    x_end()
    lax.fori_loop(0, g_ref.shape[1] // 256, product, 0)
    theirs = kv_ref.at[:, :, :, 1 - me.core]
    ours = kv_ref.at[:, :, :, me.core]
    arrived(theirs, mate_send, mate_recv, mate)
    pltpu.make_async_remote_copy(
        src_ref=ours, dst_ref=ours, send_sem=mate_send, recv_sem=mate_recv,
        device_id=mate, device_id_type=MESH,
    ).wait_send()
    own_copy.wait()


def gather(k, v, da, w):
    return pl.pallas_call(
        gather_kernel,
        out_shape=(
            pltpu.VMEM(PIECES, BF16),
            pltpu.VMEM((ROWS, w.shape[0]), BF16),
        ),
        in_specs=[VMEM, VMEM, VMEM, ANY],
        out_specs=(ANY, VMEM),
        scratch_shapes=[
            pltpu.VMEM((ROWS, 2 * D), BF16),
            pltpu.VMEM((4,) + da.shape, BF16),
            pltpu.VMEM(w.shape, BF16),
            pltpu.SemaphoreType.DMA((2,)),
            pltpu.SemaphoreType.DMA((48,)),
            pltpu.SemaphoreType.DMA((32,)),
            pltpu.SemaphoreType.DMA,
            pltpu.SemaphoreType.DMA,
            pltpu.SemaphoreType.DMA((4,)),
            pltpu.SemaphoreType.DMA((4,)),
        ],
        compiler_params=pltpu.CompilerParams(
            collective_id=0, has_side_effects=True, vmem_limit_bytes=GATHER_VMEM
        ),
        name="gather",
    )(k, v, da, w)


def attention_kernel(
    seq_ref, order_ref, seg_ref, q_ref, g_ref, kv, o_ref, dq_ref, dkv_ref,
    stored, qs, gs, q_t, g_t, scores, weights, d_scores, acc,
):
    seq = seq_ref[0]
    for r in range(SPANS):
        stored[order_ref[r]] = r
    seg = seg_ref[...]
    starts = [jnp.sum((seg < d).astype(jnp.int32)) for d in range(1, 8)]
    dkv_ref[...] = jnp.zeros_like(dkv_ref)
    key_iota = lax.broadcasted_iota(jnp.int32, (CHUNK, QROWS), 0)
    lane = lax.broadcasted_iota(jnp.int32, (1, QROWS), 1)

    def begin(position):
        first = jnp.zeros_like(position)
        for start in starts:
            first = jnp.maximum(first, jnp.where(start <= position, start, 0))
        return first

    def one_span(half, _):
        row = pl.multiple_of(half * SPAN, SPAN)
        span = order_ref[seq * 2 + half]
        position = span * SPAN + lax.rem(lane, SPAN)
        first = begin(position)
        span_0 = lax.div(begin(span * SPAN), SPAN)
        units = lax.div(span - span_0 + UNIT, UNIT)
        for h in range(HEADS):
            qs[h * SPAN:(h + 1) * SPAN, :] = q_ref[pl.ds(row, SPAN), h * D:(h + 1) * D]
            gs[h * SPAN:(h + 1) * SPAN, :] = g_ref[pl.ds(row, SPAN), h * D:(h + 1) * D]
        q_t[...] = qs[...].T
        g_t[...] = gs[...].T

        def tiles(step, carried):
            done = 0
            for size in SIZES:
                count = lax.div(units - done, size)
                carried = lax.fori_loop(
                    0, count,
                    lambda i, c, size=size, done=done: step(
                        (done + i * size) * UNIT, size * UNIT, c
                    ),
                    carried,
                )
                done = done + count * size
            return carried

        def rows_of(at, count):
            return [
                pl.multiple_of(stored[jnp.minimum(span_0 + at + b, SPANS - 1)] * SPAN, SPAN)
                for b in range(count)
            ]

        def load(rows, column):
            return jnp.concatenate(
                [kv[pl.ds(r, SPAN), column * D:(column + 1) * D] for r in rows], axis=0
            )

        def keys(at, offset, size):
            return pl.ds(pl.multiple_of(at * SPAN, SPAN) + offset, size)

        per = CHUNK // SPAN

        def score(at, count, best):
            rows = rows_of(at, count)
            base = (span_0 + at) * SPAN
            low, high = first - base, position - base
            for c in range(count // per):
                raw = jnp.dot(
                    load(rows[c * per:(c + 1) * per], 0), q_t[...], preferred_element_type=F32
                )
                place = key_iota + c * CHUNK
                raw = jnp.where((place >= low) & (place <= high), raw, -1e30)
                scores[keys(at, c * CHUNK, CHUNK), :] = raw
                best = jnp.maximum(best, jnp.max(raw.reshape(CHUNK // 8, 8, QROWS), axis=0))
            return best

        best = tiles(score, jnp.full((8, QROWS), -1e30, F32))
        top = jnp.max(best, axis=0, keepdims=True) * EXP2_SCALE
        acc[...] = jnp.zeros_like(acc)

        def forward(at, count, total):
            rows = rows_of(at, count)
            for u in range(count // PER_MIX):
                parts = []
                for c in range(u * PER_MIX // per, (u + 1) * PER_MIX // per):
                    part = keys(at, c * CHUNK, CHUNK)
                    exponent = jnp.exp2(scores[part, :] * EXP2_SCALE - top)
                    rounded = exponent.astype(BF16)
                    weights[part, :] = rounded
                    parts.append(rounded)
                    total = total + jnp.sum(exponent.reshape(CHUNK // 8, 8, QROWS), axis=0)
                acc[...] += lax.dot_general(
                    load(rows[u * PER_MIX:(u + 1) * PER_MIX], 1),
                    jnp.concatenate(parts, axis=0),
                    (((0,), (0,)), ((), ())), preferred_element_type=F32,
                )
            return total

        total = tiles(forward, jnp.zeros((8, QROWS), F32))
        inverse = 1.0 / jnp.sum(total, axis=0, keepdims=True)
        attended_t = (acc[...] * inverse).astype(BF16)
        attended = attended_t.T
        for h in range(HEADS):
            o_ref[pl.ds(row, SPAN), h * D:(h + 1) * D] = attended[h * SPAN:(h + 1) * SPAN, :]
        shrunk = (g_t[...].astype(F32) * inverse).astype(BF16)
        g_t[...] = shrunk
        gs[...] = shrunk.T
        delta = jnp.sum(
            attended_t.astype(F32) * shrunk.astype(F32), axis=0, keepdims=True
        )
        acc[...] = jnp.zeros_like(acc)

        def backward(at, count, carried):
            rows = rows_of(at, count)
            step = SLOPE // SPAN
            for c in range(count // step):
                d_prob = jnp.dot(
                    load(rows[c * step:(c + 1) * step], 1), g_t[...], preferred_element_type=F32
                )
                weight = weights[keys(at, c * SLOPE, SLOPE), :].astype(F32)
                d_scores[c * SLOPE:(c + 1) * SLOPE, :] = (weight * (d_prob - delta)).astype(BF16)
            acc[...] += lax.dot_general(
                load(rows, 0), d_scores[:count * SPAN, :], (((0,), (0,)), ((), ())),
                preferred_element_type=F32,
            )
            for c in range(count // PER_SUM):
                part = slice(c * PER_SUM * SPAN, (c + 1) * PER_SUM * SPAN)
                dk = jnp.dot(d_scores[part, :], qs[...], preferred_element_type=F32)
                dv = jnp.dot(
                    weights[keys(at, c * PER_SUM * SPAN, PER_SUM * SPAN), :], gs[...],
                    preferred_element_type=F32,
                )
                for b, r in enumerate(rows[c * PER_SUM:(c + 1) * PER_SUM]):
                    for column, terms in enumerate((dk, dv)):
                        place = (pl.ds(r, SPAN), slice(column * D, (column + 1) * D))
                        dkv_ref[place] = (
                            dkv_ref[place].astype(F32) + terms[b * SPAN:(b + 1) * SPAN, :]
                        ).astype(BF16)
            return carried

        tiles(backward, 0)
        dq = (acc[...] * SCALE).astype(BF16).T
        for h in range(HEADS):
            dq_ref[pl.ds(row, SPAN), h * D:(h + 1) * D] = dq[h * SPAN:(h + 1) * SPAN, :]
        return 0

    lax.fori_loop(0, 2, one_span, 0)


def attention(seq, order, seg, q, g, kv):
    return pl.pallas_call(
        attention_kernel,
        out_shape=(
            jax.ShapeDtypeStruct(q.shape, BF16),
            jax.ShapeDtypeStruct(q.shape, BF16),
            jax.ShapeDtypeStruct(kv.shape, BF16),
        ),
        in_specs=[SMEM, SMEM, VMEM, VMEM, VMEM, VMEM],
        out_specs=(VMEM, VMEM, VMEM),
        scratch_shapes=[
            pltpu.SMEM((SPANS,), jnp.int32),
            pltpu.VMEM((QROWS, D), BF16),
            pltpu.VMEM((QROWS, D), BF16),
            pltpu.VMEM((D, QROWS), BF16),
            pltpu.VMEM((D, QROWS), BF16),
            pltpu.VMEM((MOST_KEYS, QROWS), F32),
            pltpu.VMEM((MOST_KEYS, QROWS), BF16),
            pltpu.VMEM((max(SIZES) * UNIT * SPAN, QROWS), BF16),
            pltpu.VMEM((D, QROWS), F32),
        ],
        compiler_params=pltpu.CompilerParams(vmem_limit_bytes=ATTENTION_VMEM),
        name="attention",
    )(seq, order, seg, q, g, kv)


SUM_ROWS = 32
FAR_FIRST = (4, 3, -3, 2, -2, 1, -1, 0)


def scatter_kernel(
    part_ref, sum_ref, mine, theirs, landed, load_sem, send_sem, recv_sem, mate_send, mate_recv
):
    me = Place()
    y, z = me.y, me.z
    mate = me.device(core=1 - me.core)

    def of_z(s):
        return (slice(None),) + me.dz(s)[1:]

    def load_z(s):
        return pltpu.make_async_copy(
            part_ref.at[of_z(s) + (0,)], mine.at[of_z(s)], load_sem.at[me.dz(s)[0]]
        )

    def load_y(s):
        py = me.dy(s)
        return pltpu.make_async_copy(part_ref.at[py, :, :, 1], mine.at[py], load_sem.at[py])

    @pl.when(me.core == 0)
    def _():
        for s in FAR_FIRST:
            load_z(s).start()

    @pl.when(me.core == 1)
    def _():
        for s in (2, 1, -1, 0):
            load_y(s).start()

    me.greet(
        [mate]
        + [me.device(y=me.dy(s)) for s in (1, -1, 2)]
        + [me.device(z=me.dz(s)) for s in (1, -1, 2, -2)]
    )
    up_z, down_z = me.device(z=me.dz(1)), me.device(z=me.dz(-1))
    up_2z, down_2z = me.device(z=me.dz(2)), me.device(z=me.dz(-2))
    up_y, down_y = me.device(y=me.dy(1)), me.device(y=me.dy(-1))
    index = FAR_FIRST.index

    def terms(py, pz, slots, store):
        at = (py,) + pz[1:]
        for slot in slots:
            arrived(landed.at[slot], mate_send.at[0], recv_sem.at[slot], mate)

        def add(step, _):
            rows = pl.ds(pl.multiple_of(step * SUM_ROWS, SUM_ROWS), SUM_ROWS)
            total = mine[at + (rows,)].astype(F32) + theirs[at + (rows,)].astype(F32)
            for slot in slots:
                total = total + landed[slot, rows].astype(F32)
            store(at, rows, total)
            return 0

        lax.fori_loop(0, ROWS // SUM_ROWS, add, 0)
        return at

    def keep(at, rows, total):
        mine[at + (rows,)] = total.astype(BF16)

    def write(at, rows, total):
        sum_ref[rows, :] = total

    def pass_on(sends, py, pz, slots, slot, device):
        at = terms(py, pz, slots, keep)
        sends(mine.at[at], landed.at[slot], recv_sem.at[slot], device)

    @pl.when(me.core == 0)
    def _():
        sends = Sends(send_sem)
        mate_sends = Sends(mate_send)
        for s in FAR_FIRST:
            at = (me.dy(2),) + me.dz(s)[1:]
            mate_sends(
                part_ref.at[at + (1,)], theirs.at[at], mate_recv.at[4 + index(s)], mate
            )
        for s in (1, -1, 0):
            py = me.dy(s)
            mate_sends(part_ref.at[py, :, :, 1], theirs.at[py], mate_recv.at[py], mate)

        def ready(s):
            load_z(s).wait()
            arrived(theirs.at[of_z(s)], mate_send.at[0], mate_recv.at[me.dz(s)[0]], mate)

        order = (0, 1, -1, 2)
        up_slot = lambda s, i: (s - 1) * 4 + order.index(i)
        down_slot = lambda s, i: 16 + (s - 1) * 4 + order.index(i)
        ready(4)
        for i in (0, -1, 1, 2):
            if i in (0, 1):
                pass_on(sends, me.dy(i), me.dz(4), (), up_slot(4, i), up_2z)
            else:
                pass_on(sends, me.dy(i), me.dz(4), (), down_slot(4, i), down_2z)
        for s in (3, 2, 1):
            ready(s)
            ready(-s)
            for i in order:
                got = (up_slot(s + 1, i),) if s < 3 else ()
                got += (up_slot(4, i),) if s == 2 and i in (0, 1) else ()
                pass_on(sends, me.dy(i), me.dz(s), got, up_slot(s, i), up_z)
                got = (down_slot(s + 1, i),) if s < 3 else ()
                got += (down_slot(4, i),) if s == 2 and i in (-1, 2) else ()
                pass_on(sends, me.dy(i), me.dz(-s), got, down_slot(s, i), down_z)
        ready(0)
        last = lambda i: (up_slot(1, i), down_slot(1, i))
        for i in (1, -1, 2):
            pass_on(
                sends, me.dy(i), z, last(i), 32 + order.index(i), me.device(y=me.dy(i))
            )
        terms(y, z, last(0) + (33, 34, 35), write)
        mate_sends.wait()
        sends.wait()

    @pl.when(me.core == 1)
    def _():
        sends = Sends(send_sem)
        mate_sends = Sends(mate_send)
        for s in FAR_FIRST:
            at = of_z(s)
            mate_sends(part_ref.at[at + (0,)], theirs.at[at], mate_recv.at[me.dz(s)[0]], mate)

        def ready(s):
            py = me.dy(s)
            load_y(s).wait()
            arrived(theirs.at[py], mate_send.at[0], mate_recv.at[py], mate)

        load_y(2).wait()
        for s in FAR_FIRST:
            at = (me.dy(2),) + me.dz(s)[1:]
            arrived(theirs.at[at], mate_send.at[0], mate_recv.at[4 + index(s)], mate)
            pass_on(sends, me.dy(2), me.dz(s), (), index(s), me.device(y=me.dy(2)))
        ready(1)
        ready(-1)
        for s in FAR_FIRST:
            pass_on(sends, me.dy(1), me.dz(s), (), 8 + index(s), up_y)
            pass_on(sends, me.dy(-1), me.dz(s), (), 16 + index(s), down_y)
        ready(0)
        routes = {
            4: ((), up_2z), 3: ((), up_z), -3: ((), down_z), 2: ((3, 4), up_2z),
            -2: ((-3,), down_2z), 1: ((), up_z), -1: ((), down_z),
        }
        for s in FAR_FIRST[:-1]:
            extra, device = routes[s]
            got = (index(s), 8 + index(s), 16 + index(s)) + tuple(24 + index(e) for e in extra)
            pass_on(sends, y, me.dz(s), got, 24 + index(s), device)
        got = (7, 15, 23) + tuple(24 + index(e) for e in (1, -1, 2, -2))
        terms(y, z, got, write)
        mate_sends.wait()
        sends.wait()


def scatter(part):
    return pl.pallas_call(
        scatter_kernel,
        out_shape=jax.ShapeDtypeStruct((ROWS, 2 * D), F32),
        in_specs=[ANY],
        out_specs=VMEM,
        scratch_shapes=[
            pltpu.VMEM((4, 2, 4, ROWS, 2 * D), BF16),
            pltpu.VMEM((4, 2, 4, ROWS, 2 * D), BF16),
            pltpu.VMEM((36, ROWS, 2 * D), BF16),
            pltpu.SemaphoreType.DMA((8,)),
            pltpu.SemaphoreType.DMA((40,)),
            pltpu.SemaphoreType.DMA((36,)),
            pltpu.SemaphoreType.DMA((12,)),
            pltpu.SemaphoreType.DMA((12,)),
        ],
        compiler_params=pltpu.CompilerParams(
            collective_id=1, has_side_effects=True, vmem_limit_bytes=SCATTER_VMEM
        ),
        name="scatter",
    )(part)


def finish_kernel(sum_ref, dk_ref, dv_ref):
    dk_ref[...] = (sum_ref[:, :D] * SCALE).astype(BF16)
    dv_ref[...] = sum_ref[:, D:].astype(BF16)


def finish(sums):
    return pl.pallas_call(
        finish_kernel,
        out_shape=(jax.ShapeDtypeStruct((ROWS, D), BF16),) * 2,
        in_specs=[VMEM],
        out_specs=(VMEM, VMEM),
        compiler_params=pltpu.CompilerParams(vmem_limit_bytes=2 * MIB),
        name="finish",
    )(sums)


def shards(
    query_matrix, key_matrix, value_matrix, segment_ids, block_order, out_weight, d_attended
):
    seq = lax.axis_index(("inner", "outer")).astype(jnp.int32).reshape(1)
    pieces, g = gather(key_matrix, value_matrix, d_attended, out_weight)
    attended, d_queries, terms = attention(
        seq, block_order, segment_ids.reshape(64, 128), query_matrix, g,
        pieces.reshape(TOKENS, 2 * D),
    )
    sums = scatter(terms.reshape(PIECES))
    key_gradient, value_gradient = finish(sums)
    return (attended, d_queries, key_gradient, value_gradient)


def solution(mesh):
    return jax.shard_map(
        shards,
        mesh=mesh,
        in_specs=(
            P(("inner", "outer"), "tensor"),
            P(("inner", "outer"), "tensor"),
            P(("inner", "outer"), "tensor"),
            P(),
            P(),
            P("tensor", None),
            P(("inner", "outer", "tensor"), None),
        ),
        out_specs=(
            P(("inner", "outer"), "tensor"),
            P(("inner", "outer"), "tensor"),
            P(("inner", "outer"), "tensor"),
            P(("inner", "outer"), "tensor"),
        ),
        check_vma=False,
    )
```

```python
import functools
import math

import jax
import jax.numpy as jnp
from jax import lax
from jax.experimental import pallas as pl
from jax.experimental.pallas import tpu as pltpu
from jax.sharding import PartitionSpec as P

D = 128
HEADS = 8
ROWS = 128
SPAN = 64
SPANS = 128
TOKENS = 8192
QROWS = SPAN * HEADS
UNIT = 8
SIZES = (4, 2, 1)
CHUNK = 128
PER_MIX, PER_SUM, SLOPE = 8, 8, 512
MOST_KEYS = (65 + UNIT - 1) // UNIT * UNIT * SPAN
SCALE = 1.0 / math.sqrt(D)
EXP2_SCALE = SCALE * math.log2(math.e)
F32 = jnp.float32
BF16 = jnp.bfloat16
MESH = pl.DeviceIdType.MESH
VMEM = pl.BlockSpec(memory_space=pltpu.VMEM)
SMEM = pl.BlockSpec(memory_space=pltpu.SMEM)
ANY = pl.BlockSpec(memory_space=pl.ANY)
MIB = 1024 * 1024
GATHER_VMEM, ATTENTION_VMEM, SCATTER_VMEM = 54 * MIB, 34 * MIB, 8 * MIB
PIECES = (4, 2, 4, 2, ROWS, 2 * D)


class Place:
    def __init__(self):
        inner, outer = lax.axis_index("inner"), lax.axis_index("outer")
        self.x = lax.axis_index("tensor")
        self.y = lax.div(inner, 2)
        self.core = lax.rem(outer, 2)
        z = lax.div(outer, 2) * 2 + lax.rem(inner, 2)
        self.ys = [lax.rem(self.y + s, 4) for s in range(4)]
        self.xs = [lax.rem(self.x + s, 4) for s in range(4)]
        zs = [lax.rem(z + s, 8) for s in range(8)]
        self.zs = [(at, lax.rem(at, 2), lax.div(at, 2)) for at in zs]
        self.z = self.zs[0]

    def dy(self, step):
        return self.ys[step % 4]

    def dz(self, step):
        return self.zs[step % 8]

    def dx(self, step):
        return self.xs[step % 4]

    def device(self, y=None, z=None, core=None, x=None):
        y = self.y if y is None else y
        z = self.z if z is None else z
        core = self.core if core is None else core
        x = self.x if x is None else x
        return (y * 2 + z[1], z[2] * 2 + core, x)

    def greet(self, devices):
        barrier = pltpu.get_barrier_semaphore()
        for device in devices:
            pl.semaphore_signal(barrier, inc=1, device_id=device, device_id_type=MESH)
        pl.semaphore_wait(barrier, len(devices))


class Sends:
    def __init__(self, sems):
        self.sems, self.copies = sems, []

    def __call__(self, src, dst, recv_sem, device):
        copy = pltpu.make_async_remote_copy(
            src_ref=src, dst_ref=dst, send_sem=self.sems.at[len(self.copies)],
            recv_sem=recv_sem, device_id=device, device_id_type=MESH,
        )
        copy.start()
        self.copies.append(copy)

    def wait(self):
        for copy in self.copies:
            copy.wait_send()
        self.copies = []


def arrived(ref, send_sem, recv_sem, device):
    pltpu.make_async_remote_copy(
        src_ref=ref, dst_ref=ref, send_sem=send_sem, recv_sem=recv_sem,
        device_id=device, device_id_type=MESH,
    ).wait_recv()


def piece(ref, y, z, *core):
    return ref.at[(y, z[1], z[2]) + core]


def gather_kernel(
    k_ref, v_ref, da_ref, w_ref, kv_ref, g_ref,
    own, da_all, w_all, local_sem, send_sem, recv_sem, mate_send, mate_recv, x_send, x_recv,
):
    me = Place()
    y, z, x = me.y, me.z, me.x
    w_copy = pltpu.make_async_copy(w_ref, w_all, local_sem.at[0])
    w_copy.start()
    own[:, :D] = k_ref[...]
    own[:, D:] = v_ref[...]
    own_copy = pltpu.make_async_copy(own, piece(kv_ref, y, z, me.core), local_sem.at[1])
    own_copy.start()
    da_all[x] = da_ref[...]
    mate = me.device(core=1 - me.core)
    me.greet(
        [mate]
        + [me.device(y=me.dy(s)) for s in (1, -1, 2)]
        + [me.device(z=me.dz(s)) for s in (1, -1, 2, -2)]
        + [me.device(x=me.dx(s)) for s in (1, -1)]
    )
    up_x, down_x = me.device(x=me.dx(1)), me.device(x=me.dx(-1))
    half = da_ref.shape[1] // 2
    x_sends = Sends(x_send)

    def x_start():
        x_sends(da_ref, da_all.at[x], x_recv.at[0], up_x)
        x_sends(da_ref, da_all.at[x], x_recv.at[1], down_x)

    def x_middle():
        low, high = me.dx(-1), me.dx(1)
        arrived(da_all.at[low], x_send.at[0], x_recv.at[0], mate)
        part = da_all.at[low, :, pl.ds(0, half)]
        x_sends(part, part, x_recv.at[2], up_x)
        arrived(da_all.at[high], x_send.at[0], x_recv.at[1], mate)
        part = da_all.at[high, :, pl.ds(half, half)]
        x_sends(part, part, x_recv.at[3], down_x)

    def x_end():
        far = me.dx(2)
        arrived(da_all.at[far, :, pl.ds(0, half)], x_send.at[0], x_recv.at[2], mate)
        arrived(da_all.at[far, :, pl.ds(half, half)], x_send.at[0], x_recv.at[3], mate)
        w_copy.wait()

    def product(at):
        width = 256
        rows = da_all[...].reshape(ROWS, da_ref.shape[1])
        g_ref[:, at * width:(at + 1) * width] = lax.dot_general(
            rows, w_all[at * width:(at + 1) * width, :], (((1,), (1,)), ((), ())),
            preferred_element_type=F32,
        ).astype(BF16)

    def to_mate(src, dst):
        pltpu.make_async_remote_copy(
            src_ref=src, dst_ref=dst, send_sem=mate_send, recv_sem=mate_recv,
            device_id=mate, device_id_type=MESH,
        ).start()

    def finish(core, sends):
        theirs = kv_ref.at[:, :, :, 1 - core]
        ours = kv_ref.at[:, :, :, core]
        arrived(theirs, mate_send, mate_recv, mate)
        pltpu.make_async_remote_copy(
            src_ref=ours, dst_ref=ours, send_sem=mate_send, recv_sem=mate_recv,
            device_id=mate, device_id_type=MESH,
        ).wait_send()
        sends.wait()
        x_sends.wait()

    up_z, down_z = me.device(z=me.dz(1)), me.device(z=me.dz(-1))
    up_2z, down_2z = me.device(z=me.dz(2)), me.device(z=me.dz(-2))
    up_y, down_y = me.device(y=me.dy(1)), me.device(y=me.dy(-1))

    def fetch(core, sends, step_y, step_z, devices, wait=True):
        py, pz = me.dy(step_y), me.dz(step_z)
        dst = piece(kv_ref, py, pz, core)
        sem = recv_sem.at[py * 8 + pz[0]]
        src = dst if wait else own
        if wait:
            arrived(dst, mate_send, sem, mate)
        for device in devices:
            sends(src, dst, sem, device)
        to_mate(src, dst)

    @pl.when(me.core == 0)
    def _():
        sends = Sends(send_sem)
        fetch(0, sends, 0, 0, [up_y, down_y, me.device(y=me.dy(2)), up_z, down_z], wait=False)
        x_start()
        for i in (1, -1, 2):
            fetch(0, sends, i, 0, [up_z, down_z])
        for i in (0, 1, -1, 2):
            fetch(0, sends, i, -1, [up_z])
            fetch(0, sends, i, 1, [down_z])
        x_middle()
        for i in (0, 1, -1, 2):
            fetch(0, sends, i, -2, [up_2z, up_z] if i in (0, 1) else [up_z])
            fetch(0, sends, i, 2, [down_2z, down_z] if i in (-1, 2) else [down_z])
        x_end()
        for at, i in enumerate((0, 1, -1, 2)):
            product(at)
            fetch(0, sends, i, -3, [])
            fetch(0, sends, i, 3, [])
        for i in (0, -1, 1, 2):
            fetch(0, sends, i, 4, [])
        finish(0, sends)

    @pl.when(me.core == 1)
    def _():
        sends = Sends(send_sem)
        fetch(1, sends, 0, 0, [up_z, down_z, up_2z, down_2z, up_y, down_y], wait=False)
        x_start()

        def across(s):
            fetch(1, sends, -1, s, [up_y] if s <= 0 else [])
            fetch(1, sends, 1, s, [down_y] if s > 0 else [])

        fetch(1, sends, 0, -1, [up_y, down_y])
        fetch(1, sends, 0, 1, [up_y, down_y])
        across(0)
        fetch(1, sends, 0, -2, [up_2z, up_z, up_y, down_y])
        fetch(1, sends, 0, 2, [down_z, up_y, down_y])
        across(-1)
        across(1)
        fetch(1, sends, 0, -3, [up_y, down_y])
        fetch(1, sends, 0, 3, [up_y, down_y])
        across(-2)
        across(2)
        fetch(1, sends, 0, 4, [up_y, down_y])
        x_middle()
        across(-3)
        across(3)
        across(4)
        x_end()
        for at in range(4):
            product(at)
            for s in ((0, -1), (1, -2), (2, -3), (3, 4))[at]:
                fetch(1, sends, 2, s, [])
        finish(1, sends)

    own_copy.wait()


def gather(k, v, da, w):
    return pl.pallas_call(
        gather_kernel,
        out_shape=(
            pltpu.VMEM(PIECES, BF16),
            pltpu.VMEM((ROWS, w.shape[0]), BF16),
        ),
        in_specs=[VMEM, VMEM, VMEM, ANY],
        out_specs=(ANY, VMEM),
        scratch_shapes=[
            pltpu.VMEM((ROWS, 2 * D), BF16),
            pltpu.VMEM((4,) + da.shape, BF16),
            pltpu.VMEM(w.shape, BF16),
            pltpu.SemaphoreType.DMA((2,)),
            pltpu.SemaphoreType.DMA((48,)),
            pltpu.SemaphoreType.DMA((32,)),
            pltpu.SemaphoreType.DMA,
            pltpu.SemaphoreType.DMA,
            pltpu.SemaphoreType.DMA((4,)),
            pltpu.SemaphoreType.DMA((4,)),
        ],
        compiler_params=pltpu.CompilerParams(
            collective_id=0, has_side_effects=True, vmem_limit_bytes=GATHER_VMEM
        ),
        name="gather",
    )(k, v, da, w)


def attention_kernel(
    seq_ref, order_ref, seg_ref, q_ref, g_ref, kv, o_ref, dq_ref, dkv_ref,
    stored, qs, gs, q_t, g_t, scores, weights, d_scores, acc,
):
    seq = seq_ref[0]
    for r in range(SPANS):
        stored[order_ref[r]] = r
    seg = seg_ref[...]
    starts = [jnp.sum((seg < d).astype(jnp.int32)) for d in range(1, 8)]
    dkv_ref[...] = jnp.zeros_like(dkv_ref)
    key_iota = lax.broadcasted_iota(jnp.int32, (CHUNK, QROWS), 0)
    lane = lax.broadcasted_iota(jnp.int32, (1, QROWS), 1)

    def begin(position):
        first = jnp.zeros_like(position)
        for start in starts:
            first = jnp.maximum(first, jnp.where(start <= position, start, 0))
        return first

    def one_span(half, _):
        row = pl.multiple_of(half * SPAN, SPAN)
        span = order_ref[seq * 2 + half]
        position = span * SPAN + lax.rem(lane, SPAN)
        first = begin(position)
        span_0 = lax.div(begin(span * SPAN), SPAN)
        units = lax.div(span - span_0 + UNIT, UNIT)
        for h in range(HEADS):
            qs[h * SPAN:(h + 1) * SPAN, :] = q_ref[pl.ds(row, SPAN), h * D:(h + 1) * D]
            gs[h * SPAN:(h + 1) * SPAN, :] = g_ref[pl.ds(row, SPAN), h * D:(h + 1) * D]
        q_t[...] = qs[...].T
        g_t[...] = gs[...].T

        def tiles(step, carried):
            done = 0
            for size in SIZES:
                count = lax.div(units - done, size)
                carried = lax.fori_loop(
                    0, count,
                    lambda i, c, size=size, done=done: step(
                        (done + i * size) * UNIT, size * UNIT, c
                    ),
                    carried,
                )
                done = done + count * size
            return carried

        def rows_of(at, count):
            return [
                pl.multiple_of(stored[jnp.minimum(span_0 + at + b, SPANS - 1)] * SPAN, SPAN)
                for b in range(count)
            ]

        def load(rows, column):
            return jnp.concatenate(
                [kv[pl.ds(r, SPAN), column * D:(column + 1) * D] for r in rows], axis=0
            )

        def keys(at, offset, size):
            return pl.ds(pl.multiple_of(at * SPAN, SPAN) + offset, size)

        per = CHUNK // SPAN

        def score(at, count, best):
            rows = rows_of(at, count)
            base = (span_0 + at) * SPAN
            low, high = first - base, position - base
            for c in range(count // per):
                raw = jnp.dot(
                    load(rows[c * per:(c + 1) * per], 0), q_t[...], preferred_element_type=F32
                )
                place = key_iota + c * CHUNK
                raw = jnp.where((place >= low) & (place <= high), raw, -1e30)
                scores[keys(at, c * CHUNK, CHUNK), :] = raw
                best = jnp.maximum(best, jnp.max(raw.reshape(CHUNK // 8, 8, QROWS), axis=0))
            return best

        best = tiles(score, jnp.full((8, QROWS), -1e30, F32))
        top = jnp.max(best, axis=0, keepdims=True) * EXP2_SCALE
        acc[...] = jnp.zeros_like(acc)

        def forward(at, count, total):
            rows = rows_of(at, count)
            for u in range(count // PER_MIX):
                parts = []
                for c in range(u * PER_MIX // per, (u + 1) * PER_MIX // per):
                    part = keys(at, c * CHUNK, CHUNK)
                    exponent = jnp.exp2(scores[part, :] * EXP2_SCALE - top)
                    rounded = exponent.astype(BF16)
                    weights[part, :] = rounded
                    parts.append(rounded)
                    total = total + jnp.sum(exponent.reshape(CHUNK // 8, 8, QROWS), axis=0)
                acc[...] += lax.dot_general(
                    load(rows[u * PER_MIX:(u + 1) * PER_MIX], 1),
                    jnp.concatenate(parts, axis=0),
                    (((0,), (0,)), ((), ())), preferred_element_type=F32,
                )
            return total

        total = tiles(forward, jnp.zeros((8, QROWS), F32))
        inverse = 1.0 / jnp.sum(total, axis=0, keepdims=True)
        attended_t = (acc[...] * inverse).astype(BF16)
        attended = attended_t.T
        for h in range(HEADS):
            o_ref[pl.ds(row, SPAN), h * D:(h + 1) * D] = attended[h * SPAN:(h + 1) * SPAN, :]
        shrunk = (g_t[...].astype(F32) * inverse).astype(BF16)
        g_t[...] = shrunk
        gs[...] = shrunk.T
        delta = jnp.sum(
            attended_t.astype(F32) * shrunk.astype(F32), axis=0, keepdims=True
        )
        acc[...] = jnp.zeros_like(acc)

        def backward(at, count, carried):
            rows = rows_of(at, count)
            step = SLOPE // SPAN
            for c in range(count // step):
                d_prob = jnp.dot(
                    load(rows[c * step:(c + 1) * step], 1), g_t[...], preferred_element_type=F32
                )
                weight = weights[keys(at, c * SLOPE, SLOPE), :].astype(F32)
                d_scores[c * SLOPE:(c + 1) * SLOPE, :] = (weight * (d_prob - delta)).astype(BF16)
            acc[...] += lax.dot_general(
                load(rows, 0), d_scores[:count * SPAN, :], (((0,), (0,)), ((), ())),
                preferred_element_type=F32,
            )
            for c in range(count // PER_SUM):
                part = slice(c * PER_SUM * SPAN, (c + 1) * PER_SUM * SPAN)
                dk = jnp.dot(d_scores[part, :], qs[...], preferred_element_type=F32)
                dv = jnp.dot(
                    weights[keys(at, c * PER_SUM * SPAN, PER_SUM * SPAN), :], gs[...],
                    preferred_element_type=F32,
                )
                for b, r in enumerate(rows[c * PER_SUM:(c + 1) * PER_SUM]):
                    for column, terms in enumerate((dk, dv)):
                        place = (pl.ds(r, SPAN), slice(column * D, (column + 1) * D))
                        dkv_ref[place] = (
                            dkv_ref[place].astype(F32) + terms[b * SPAN:(b + 1) * SPAN, :]
                        ).astype(BF16)
            return carried

        tiles(backward, 0)
        dq = (acc[...] * SCALE).astype(BF16).T
        for h in range(HEADS):
            dq_ref[pl.ds(row, SPAN), h * D:(h + 1) * D] = dq[h * SPAN:(h + 1) * SPAN, :]
        return 0

    lax.fori_loop(0, 2, one_span, 0)


def attention(seq, order, seg, q, g, kv):
    return pl.pallas_call(
        attention_kernel,
        out_shape=(
            jax.ShapeDtypeStruct(q.shape, BF16),
            jax.ShapeDtypeStruct(q.shape, BF16),
            jax.ShapeDtypeStruct(kv.shape, BF16),
        ),
        in_specs=[SMEM, SMEM, VMEM, VMEM, VMEM, VMEM],
        out_specs=(VMEM, VMEM, VMEM),
        scratch_shapes=[
            pltpu.SMEM((SPANS,), jnp.int32),
            pltpu.VMEM((QROWS, D), BF16),
            pltpu.VMEM((QROWS, D), BF16),
            pltpu.VMEM((D, QROWS), BF16),
            pltpu.VMEM((D, QROWS), BF16),
            pltpu.VMEM((MOST_KEYS, QROWS), F32),
            pltpu.VMEM((MOST_KEYS, QROWS), BF16),
            pltpu.VMEM((max(SIZES) * UNIT * SPAN, QROWS), BF16),
            pltpu.VMEM((D, QROWS), F32),
        ],
        compiler_params=pltpu.CompilerParams(vmem_limit_bytes=ATTENTION_VMEM),
        name="attention",
    )(seq, order, seg, q, g, kv)


SUM_ROWS = 32
SPLIT = 64
FAR_FIRST = (4, 3, -3, 2, -2, 1, -1, 0)
UPWARD = (4, -3, 2, -1)
Z_SLOTS = 36


def scatter_kernel(
    part_ref, sum_ref, mine, theirs, landed, load_sem, send_sem, recv_sem, mate_send, mate_recv
):
    me = Place()
    y, z = me.y, me.z
    mate = me.device(core=1 - me.core)

    def of_z(s):
        return (slice(None),) + me.dz(s)[1:]

    def load_z(s):
        return pltpu.make_async_copy(
            part_ref.at[of_z(s) + (0,)], mine.at[of_z(s)], load_sem.at[me.dz(s)[0]]
        )

    def load_y(s):
        py = me.dy(s)
        return pltpu.make_async_copy(part_ref.at[py, :, :, 1], mine.at[py], load_sem.at[py])

    @pl.when(me.core == 0)
    def _():
        for s in FAR_FIRST:
            load_z(s).start()

    @pl.when(me.core == 1)
    def _():
        for s in (2, 1, -1, 0):
            load_y(s).start()

    me.greet(
        [mate]
        + [me.device(y=me.dy(s)) for s in (1, -1, 2)]
        + [me.device(z=me.dz(s)) for s in (1, -1, 2, -2)]
    )
    up_z, down_z = me.device(z=me.dz(1)), me.device(z=me.dz(-1))
    up_2z, down_2z = me.device(z=me.dz(2)), me.device(z=me.dz(-2))
    up_y, down_y = me.device(y=me.dy(1)), me.device(y=me.dy(-1))
    index = FAR_FIRST.index

    def keep(at, rows, total):
        mine[at + (rows,)] = total.astype(BF16)

    def write(at, rows, total):
        sum_ref[rows, :] = total

    class Route:
        def __init__(self, sends, start, size, first_sem):
            self.sends, self.start, self.size, self.first_sem = sends, start, size, first_sem

        def slot(self, slot):
            return landed.at[slot, pl.ds(self.start, self.size)]

        def terms(self, py, pz, slots, store):
            at = (py,) + pz[1:]
            for slot in slots:
                arrived(
                    self.slot(slot), mate_send.at[0], recv_sem.at[self.first_sem + slot], mate
                )

            def add(step, _):
                first = pl.multiple_of(self.start + step * SUM_ROWS, SUM_ROWS)
                rows = pl.ds(first, SUM_ROWS)
                total = mine[at + (rows,)].astype(F32) + theirs[at + (rows,)].astype(F32)
                for slot in slots:
                    total = total + landed[slot, rows].astype(F32)
                store(at, rows, total)
                return 0

            lax.fori_loop(0, self.size // SUM_ROWS, add, 0)
            return at

        def pass_on(self, py, pz, slots, slot, device):
            at = self.terms(py, pz, slots, keep)
            self.sends(
                mine.at[at + (pl.ds(self.start, self.size),)], self.slot(slot),
                recv_sem.at[self.first_sem + slot], device,
            )

    def y_far(route, s):
        device = up_y if s in UPWARD else down_y
        route.pass_on(me.dy(2), me.dz(s), (), index(s), device)

    def y_near(route, s):
        got = (index(s),)
        up, down = (got, ()) if s in UPWARD else ((), got)
        route.pass_on(me.dy(1), me.dz(s), up, 8 + index(s), up_y)
        route.pass_on(me.dy(-1), me.dz(s), down, 16 + index(s), down_y)

    def along_z(route, s):
        extra, device = {
            4: ((), up_2z), 3: ((), up_z), -3: ((), down_z), 2: ((3, 4), up_2z),
            -2: ((-3,), down_2z), 1: ((), up_z), -1: ((), down_z),
        }[s]
        got = (8 + index(s), 16 + index(s)) + tuple(24 + index(e) for e in extra)
        route.pass_on(y, me.dz(s), got, 24 + index(s), device)

    def y_last(route):
        got = (15, 23) + tuple(24 + index(e) for e in (1, -1, 2, -2))
        route.terms(y, z, got, write)

    @pl.when(me.core == 0)
    def _():
        sends = Sends(send_sem)
        mate_sends = Sends(mate_send)
        by_z = Route(sends, 0, SPLIT, 0)
        by_y = Route(sends, SPLIT, ROWS - SPLIT, Z_SLOTS)
        for s in FAR_FIRST:
            at = (me.dy(2),) + me.dz(s)[1:]
            mate_sends(
                part_ref.at[at + (1,)], theirs.at[at], mate_recv.at[4 + index(s)], mate
            )
        for s in (1, -1, 0):
            py = me.dy(s)
            mate_sends(part_ref.at[py, :, :, 1], theirs.at[py], mate_recv.at[py], mate)

        def ready(s):
            load_z(s).wait()
            arrived(theirs.at[of_z(s)], mate_send.at[0], mate_recv.at[me.dz(s)[0]], mate)

        order = (0, 1, -1, 2)
        up_slot = lambda s, i: (s - 1) * 4 + order.index(i)
        down_slot = lambda s, i: 16 + (s - 1) * 4 + order.index(i)

        def z_step(s):
            for i in order:
                got = (up_slot(s + 1, i),) if s < 3 else ()
                got += (up_slot(4, i),) if s == 2 and i in (0, 1) else ()
                by_z.pass_on(me.dy(i), me.dz(s), got, up_slot(s, i), up_z)
                got = (down_slot(s + 1, i),) if s < 3 else ()
                got += (down_slot(4, i),) if s == 2 and i in (-1, 2) else ()
                by_z.pass_on(me.dy(i), me.dz(-s), got, down_slot(s, i), down_z)

        ready(4)
        for i in (0, -1, 1, 2):
            if i in (0, 1):
                by_z.pass_on(me.dy(i), me.dz(4), (), up_slot(4, i), up_2z)
            else:
                by_z.pass_on(me.dy(i), me.dz(4), (), down_slot(4, i), down_2z)
        y_far(by_y, 4)
        ready(3)
        ready(-3)
        z_step(3)
        for s in (3, -3):
            y_far(by_y, s)
        ready(2)
        ready(-2)
        for s in (2, -2):
            y_far(by_y, s)
        y_near(by_y, 4)
        z_step(2)
        ready(1)
        ready(-1)
        for s in (1, -1):
            y_far(by_y, s)
        for s in (3, -3):
            y_near(by_y, s)
        ready(0)
        y_far(by_y, 0)
        z_step(1)
        for s in (2, -2, 1, -1, 0):
            y_near(by_y, s)
        for s in (4, 3, -3):
            along_z(by_y, s)
        last = lambda i: (up_slot(1, i), down_slot(1, i))
        for i in (1, -1, 2):
            by_z.pass_on(me.dy(i), z, last(i), 32 + order.index(i), me.device(y=me.dy(i)))
        for s in (1, -1, 2, -2):
            along_z(by_y, s)
        by_z.terms(y, z, last(0) + (33, 34, 35), write)
        y_last(by_y)
        mate_sends.wait()
        sends.wait()

    @pl.when(me.core == 1)
    def _():
        sends = Sends(send_sem)
        mate_sends = Sends(mate_send)
        by_y = Route(sends, 0, ROWS, Z_SLOTS)
        for s in FAR_FIRST:
            at = of_z(s)
            mate_sends(part_ref.at[at + (0,)], theirs.at[at], mate_recv.at[me.dz(s)[0]], mate)

        def ready(s):
            py = me.dy(s)
            load_y(s).wait()
            arrived(theirs.at[py], mate_send.at[0], mate_recv.at[py], mate)

        load_y(2).wait()
        for s in FAR_FIRST:
            at = (me.dy(2),) + me.dz(s)[1:]
            arrived(theirs.at[at], mate_send.at[0], mate_recv.at[4 + index(s)], mate)
            y_far(by_y, s)
        ready(1)
        ready(-1)
        for s in FAR_FIRST:
            y_near(by_y, s)
        ready(0)
        for s in FAR_FIRST[:-1]:
            along_z(by_y, s)
        y_last(by_y)
        mate_sends.wait()
        sends.wait()


def scatter(part):
    return pl.pallas_call(
        scatter_kernel,
        out_shape=jax.ShapeDtypeStruct((ROWS, 2 * D), F32),
        in_specs=[ANY],
        out_specs=VMEM,
        scratch_shapes=[
            pltpu.VMEM((4, 2, 4, ROWS, 2 * D), BF16),
            pltpu.VMEM((4, 2, 4, ROWS, 2 * D), BF16),
            pltpu.VMEM((36, ROWS, 2 * D), BF16),
            pltpu.SemaphoreType.DMA((8,)),
            pltpu.SemaphoreType.DMA((64,)),
            pltpu.SemaphoreType.DMA((Z_SLOTS + 32,)),
            pltpu.SemaphoreType.DMA((12,)),
            pltpu.SemaphoreType.DMA((12,)),
        ],
        compiler_params=pltpu.CompilerParams(
            collective_id=1, has_side_effects=True, vmem_limit_bytes=SCATTER_VMEM
        ),
        name="scatter",
    )(part)


def finish_kernel(sum_ref, dk_ref, dv_ref):
    dk_ref[...] = (sum_ref[:, :D] * SCALE).astype(BF16)
    dv_ref[...] = sum_ref[:, D:].astype(BF16)


def finish(sums):
    return pl.pallas_call(
        finish_kernel,
        out_shape=(jax.ShapeDtypeStruct((ROWS, D), BF16),) * 2,
        in_specs=[VMEM],
        out_specs=(VMEM, VMEM),
        compiler_params=pltpu.CompilerParams(vmem_limit_bytes=2 * MIB),
        name="finish",
    )(sums)


def shards(
    query_matrix, key_matrix, value_matrix, segment_ids, block_order, out_weight, d_attended
):
    seq = lax.axis_index(("inner", "outer")).astype(jnp.int32).reshape(1)
    pieces, g = gather(key_matrix, value_matrix, d_attended, out_weight)
    attended, d_queries, terms = attention(
        seq, block_order, segment_ids.reshape(64, 128), query_matrix, g,
        pieces.reshape(TOKENS, 2 * D),
    )
    sums = scatter(terms.reshape(PIECES))
    key_gradient, value_gradient = finish(sums)
    return (attended, d_queries, key_gradient, value_gradient)


def solution(mesh):
    return jax.shard_map(
        shards,
        mesh=mesh,
        in_specs=(
            P(("inner", "outer"), "tensor"),
            P(("inner", "outer"), "tensor"),
            P(("inner", "outer"), "tensor"),
            P(),
            P(),
            P("tensor", None),
            P(("inner", "outer", "tensor"), None),
        ),
        out_specs=(
            P(("inner", "outer"), "tensor"),
            P(("inner", "outer"), "tensor"),
            P(("inner", "outer"), "tensor"),
            P(("inner", "outer"), "tensor"),
        ),
        check_vma=False,
    )
```

```python
import functools
import math

import jax
import jax.numpy as jnp
from jax import lax
from jax.experimental import pallas as pl
from jax.experimental.pallas import tpu as pltpu
from jax.sharding import PartitionSpec as P

D = 128
HEADS = 8
ROWS = 128
SPAN = 64
SPANS = 128
TOKENS = 8192
QROWS = SPAN * HEADS
UNIT = 8
SIZES = (4, 2, 1)
CHUNK = 128
PER_MIX, PER_SUM, SLOPE = 8, 8, 512
MOST_KEYS = (65 + UNIT - 1) // UNIT * UNIT * SPAN
SCALE = 1.0 / math.sqrt(D)
EXP2_SCALE = SCALE * math.log2(math.e)
F32 = jnp.float32
BF16 = jnp.bfloat16
MESH = pl.DeviceIdType.MESH
VMEM = pl.BlockSpec(memory_space=pltpu.VMEM)
SMEM = pl.BlockSpec(memory_space=pltpu.SMEM)
ANY = pl.BlockSpec(memory_space=pl.ANY)
MIB = 1024 * 1024
GATHER_VMEM, ATTENTION_VMEM, SCATTER_VMEM = 54 * MIB, 34 * MIB, 8 * MIB
PIECES = (4, 2, 4, 2, ROWS, 2 * D)


class Place:
    def __init__(self):
        inner, outer = lax.axis_index("inner"), lax.axis_index("outer")
        self.x = lax.axis_index("tensor")
        self.y = lax.div(inner, 2)
        self.core = lax.rem(outer, 2)
        z = lax.div(outer, 2) * 2 + lax.rem(inner, 2)
        self.ys = [lax.rem(self.y + s, 4) for s in range(4)]
        self.xs = [lax.rem(self.x + s, 4) for s in range(4)]
        zs = [lax.rem(z + s, 8) for s in range(8)]
        self.zs = [(at, lax.rem(at, 2), lax.div(at, 2)) for at in zs]
        self.z = self.zs[0]

    def dy(self, step):
        return self.ys[step % 4]

    def dz(self, step):
        return self.zs[step % 8]

    def dx(self, step):
        return self.xs[step % 4]

    def device(self, y=None, z=None, core=None, x=None):
        y = self.y if y is None else y
        z = self.z if z is None else z
        core = self.core if core is None else core
        x = self.x if x is None else x
        return (y * 2 + z[1], z[2] * 2 + core, x)

    def greet(self, devices):
        barrier = pltpu.get_barrier_semaphore()
        for device in devices:
            pl.semaphore_signal(barrier, inc=1, device_id=device, device_id_type=MESH)
        pl.semaphore_wait(barrier, len(devices))


class Sends:
    def __init__(self, sems):
        self.sems, self.copies = sems, []

    def __call__(self, src, dst, recv_sem, device):
        copy = pltpu.make_async_remote_copy(
            src_ref=src, dst_ref=dst, send_sem=self.sems.at[len(self.copies)],
            recv_sem=recv_sem, device_id=device, device_id_type=MESH,
        )
        copy.start()
        self.copies.append(copy)

    def wait(self):
        for copy in self.copies:
            copy.wait_send()
        self.copies = []


def arrived(ref, send_sem, recv_sem, device):
    pltpu.make_async_remote_copy(
        src_ref=ref, dst_ref=ref, send_sem=send_sem, recv_sem=recv_sem,
        device_id=device, device_id_type=MESH,
    ).wait_recv()


def piece(ref, y, z, *core):
    return ref.at[(y, z[1], z[2]) + core]


def gather_kernel(
    k_ref, v_ref, da_ref, w_ref, kv_ref, g_ref,
    own, da_all, w_all, local_sem, send_sem, recv_sem, mate_send, mate_recv, x_send, x_recv,
):
    me = Place()
    y, z, x = me.y, me.z, me.x
    w_copy = pltpu.make_async_copy(w_ref, w_all, local_sem.at[0])
    w_copy.start()
    own[:, :D] = k_ref[...]
    own[:, D:] = v_ref[...]
    own_copy = pltpu.make_async_copy(own, piece(kv_ref, y, z, me.core), local_sem.at[1])
    own_copy.start()
    da_all[x] = da_ref[...]
    mate = me.device(core=1 - me.core)
    me.greet(
        [mate]
        + [me.device(y=me.dy(s)) for s in (1, -1, 2)]
        + [me.device(z=me.dz(s)) for s in (1, -1, 2, -2)]
        + [me.device(x=me.dx(s)) for s in (1, -1)]
    )
    up_x, down_x = me.device(x=me.dx(1)), me.device(x=me.dx(-1))
    half = da_ref.shape[1] // 2
    x_sends = Sends(x_send)

    def x_start():
        x_sends(da_ref, da_all.at[x], x_recv.at[0], up_x)
        x_sends(da_ref, da_all.at[x], x_recv.at[1], down_x)

    def x_middle():
        low, high = me.dx(-1), me.dx(1)
        arrived(da_all.at[low], x_send.at[0], x_recv.at[0], mate)
        part = da_all.at[low, :, pl.ds(0, half)]
        x_sends(part, part, x_recv.at[2], up_x)
        arrived(da_all.at[high], x_send.at[0], x_recv.at[1], mate)
        part = da_all.at[high, :, pl.ds(half, half)]
        x_sends(part, part, x_recv.at[3], down_x)

    def x_end():
        far = me.dx(2)
        arrived(da_all.at[far, :, pl.ds(0, half)], x_send.at[0], x_recv.at[2], mate)
        arrived(da_all.at[far, :, pl.ds(half, half)], x_send.at[0], x_recv.at[3], mate)
        w_copy.wait()

    def product(at):
        width = 256
        rows = da_all[...].reshape(ROWS, da_ref.shape[1])
        g_ref[:, at * width:(at + 1) * width] = lax.dot_general(
            rows, w_all[at * width:(at + 1) * width, :], (((1,), (1,)), ((), ())),
            preferred_element_type=F32,
        ).astype(BF16)

    def to_mate(src, dst):
        pltpu.make_async_remote_copy(
            src_ref=src, dst_ref=dst, send_sem=mate_send, recv_sem=mate_recv,
            device_id=mate, device_id_type=MESH,
        ).start()

    def finish(core, sends):
        theirs = kv_ref.at[:, :, :, 1 - core]
        ours = kv_ref.at[:, :, :, core]
        arrived(theirs, mate_send, mate_recv, mate)
        pltpu.make_async_remote_copy(
            src_ref=ours, dst_ref=ours, send_sem=mate_send, recv_sem=mate_recv,
            device_id=mate, device_id_type=MESH,
        ).wait_send()
        sends.wait()
        x_sends.wait()

    up_z, down_z = me.device(z=me.dz(1)), me.device(z=me.dz(-1))
    up_2z, down_2z = me.device(z=me.dz(2)), me.device(z=me.dz(-2))
    up_y, down_y = me.device(y=me.dy(1)), me.device(y=me.dy(-1))

    def fetch(core, sends, step_y, step_z, devices, wait=True):
        py, pz = me.dy(step_y), me.dz(step_z)
        dst = piece(kv_ref, py, pz, core)
        sem = recv_sem.at[py * 8 + pz[0]]
        src = dst if wait else own
        if wait:
            arrived(dst, mate_send, sem, mate)
        for device in devices:
            sends(src, dst, sem, device)
        to_mate(src, dst)

    @pl.when(me.core == 0)
    def _():
        sends = Sends(send_sem)
        fetch(0, sends, 0, 0, [up_y, down_y, me.device(y=me.dy(2)), up_z, down_z], wait=False)
        x_start()
        for i in (1, -1, 2):
            fetch(0, sends, i, 0, [up_z, down_z])
        for i in (0, 1, -1, 2):
            fetch(0, sends, i, -1, [up_z])
            fetch(0, sends, i, 1, [down_z])
        x_middle()
        for i in (0, 1, -1, 2):
            fetch(0, sends, i, -2, [up_2z, up_z] if i in (0, 1) else [up_z])
            fetch(0, sends, i, 2, [down_2z, down_z] if i in (-1, 2) else [down_z])
        x_end()
        for at, i in enumerate((0, 1, -1, 2)):
            product(at)
            fetch(0, sends, i, -3, [])
            fetch(0, sends, i, 3, [])
        for i in (0, -1, 1, 2):
            fetch(0, sends, i, 4, [])
        finish(0, sends)

    @pl.when(me.core == 1)
    def _():
        sends = Sends(send_sem)
        fetch(1, sends, 0, 0, [up_z, down_z, up_2z, down_2z, up_y, down_y], wait=False)
        x_start()

        def across(s):
            fetch(1, sends, -1, s, [up_y] if s <= 0 else [])
            fetch(1, sends, 1, s, [down_y] if s > 0 else [])

        fetch(1, sends, 0, -1, [up_y, down_y])
        fetch(1, sends, 0, 1, [up_y, down_y])
        across(0)
        fetch(1, sends, 0, -2, [up_2z, up_z, up_y, down_y])
        fetch(1, sends, 0, 2, [down_z, up_y, down_y])
        across(-1)
        across(1)
        fetch(1, sends, 0, -3, [up_y, down_y])
        fetch(1, sends, 0, 3, [up_y, down_y])
        across(-2)
        across(2)
        fetch(1, sends, 0, 4, [up_y, down_y])
        x_middle()
        across(-3)
        across(3)
        across(4)
        x_end()
        for at in range(4):
            product(at)
            for s in ((0, -1), (1, -2), (2, -3), (3, 4))[at]:
                fetch(1, sends, 2, s, [])
        finish(1, sends)

    own_copy.wait()


def gather(k, v, da, w):
    return pl.pallas_call(
        gather_kernel,
        out_shape=(
            pltpu.VMEM(PIECES, BF16),
            pltpu.VMEM((ROWS, w.shape[0]), BF16),
        ),
        in_specs=[VMEM, VMEM, VMEM, ANY],
        out_specs=(ANY, VMEM),
        scratch_shapes=[
            pltpu.VMEM((ROWS, 2 * D), BF16),
            pltpu.VMEM((4,) + da.shape, BF16),
            pltpu.VMEM(w.shape, BF16),
            pltpu.SemaphoreType.DMA((2,)),
            pltpu.SemaphoreType.DMA((48,)),
            pltpu.SemaphoreType.DMA((32,)),
            pltpu.SemaphoreType.DMA,
            pltpu.SemaphoreType.DMA,
            pltpu.SemaphoreType.DMA((4,)),
            pltpu.SemaphoreType.DMA((4,)),
        ],
        compiler_params=pltpu.CompilerParams(
            collective_id=0, has_side_effects=True, vmem_limit_bytes=GATHER_VMEM
        ),
        name="gather",
    )(k, v, da, w)


def attention_kernel(
    seq_ref, order_ref, seg_ref, q_ref, g_ref, kv, o_ref, dq_ref, dkv_ref,
    stored, qs, gs, q_t, g_t, scores, weights, d_scores, acc,
):
    seq = seq_ref[0]
    for r in range(SPANS):
        stored[order_ref[r]] = r
    seg = seg_ref[...]
    starts = [jnp.sum((seg < d).astype(jnp.int32)) for d in range(1, 8)]
    dkv_ref[...] = jnp.zeros_like(dkv_ref)
    key_iota = lax.broadcasted_iota(jnp.int32, (CHUNK, QROWS), 0)
    lane = lax.broadcasted_iota(jnp.int32, (1, QROWS), 1)

    def begin(position):
        first = jnp.zeros_like(position)
        for start in starts:
            first = jnp.maximum(first, jnp.where(start <= position, start, 0))
        return first

    def one_span(half, _):
        row = pl.multiple_of(half * SPAN, SPAN)
        span = order_ref[seq * 2 + half]
        position = span * SPAN + lax.rem(lane, SPAN)
        first = begin(position)
        span_0 = lax.div(begin(span * SPAN), SPAN)
        units = lax.div(span - span_0 + UNIT, UNIT)
        for h in range(HEADS):
            qs[h * SPAN:(h + 1) * SPAN, :] = q_ref[pl.ds(row, SPAN), h * D:(h + 1) * D]
            gs[h * SPAN:(h + 1) * SPAN, :] = g_ref[pl.ds(row, SPAN), h * D:(h + 1) * D]
        q_t[...] = qs[...].T
        g_t[...] = gs[...].T

        def tiles(step, carried):
            done = 0
            for size in SIZES:
                count = lax.div(units - done, size)
                carried = lax.fori_loop(
                    0, count,
                    lambda i, c, size=size, done=done: step(
                        (done + i * size) * UNIT, size * UNIT, c
                    ),
                    carried,
                )
                done = done + count * size
            return carried

        def rows_of(at, count):
            return [
                pl.multiple_of(stored[jnp.minimum(span_0 + at + b, SPANS - 1)] * SPAN, SPAN)
                for b in range(count)
            ]

        def load(rows, column):
            return jnp.concatenate(
                [kv[pl.ds(r, SPAN), column * D:(column + 1) * D] for r in rows], axis=0
            )

        def keys(at, offset, size):
            return pl.ds(pl.multiple_of(at * SPAN, SPAN) + offset, size)

        per = CHUNK // SPAN

        def score(at, count, best):
            rows = rows_of(at, count)
            base = (span_0 + at) * SPAN
            low, high = first - base, position - base
            for c in range(count // per):
                raw = jnp.dot(
                    load(rows[c * per:(c + 1) * per], 0), q_t[...], preferred_element_type=F32
                )
                place = key_iota + c * CHUNK
                raw = jnp.where((place >= low) & (place <= high), raw, -1e30)
                scores[keys(at, c * CHUNK, CHUNK), :] = raw
                best = jnp.maximum(best, jnp.max(raw.reshape(CHUNK // 8, 8, QROWS), axis=0))
            return best

        best = tiles(score, jnp.full((8, QROWS), -1e30, F32))
        top = jnp.max(best, axis=0, keepdims=True) * EXP2_SCALE
        acc[...] = jnp.zeros_like(acc)

        def forward(at, count, total):
            rows = rows_of(at, count)
            for u in range(count // PER_MIX):
                parts = []
                for c in range(u * PER_MIX // per, (u + 1) * PER_MIX // per):
                    part = keys(at, c * CHUNK, CHUNK)
                    exponent = jnp.exp2(scores[part, :] * EXP2_SCALE - top)
                    rounded = exponent.astype(BF16)
                    weights[part, :] = rounded
                    parts.append(rounded)
                    total = total + jnp.sum(exponent.reshape(CHUNK // 8, 8, QROWS), axis=0)
                acc[...] += lax.dot_general(
                    load(rows[u * PER_MIX:(u + 1) * PER_MIX], 1),
                    jnp.concatenate(parts, axis=0),
                    (((0,), (0,)), ((), ())), preferred_element_type=F32,
                )
            return total

        total = tiles(forward, jnp.zeros((8, QROWS), F32))
        inverse = 1.0 / jnp.sum(total, axis=0, keepdims=True)
        attended_t = (acc[...] * inverse).astype(BF16)
        attended = attended_t.T
        for h in range(HEADS):
            o_ref[pl.ds(row, SPAN), h * D:(h + 1) * D] = attended[h * SPAN:(h + 1) * SPAN, :]
        shrunk = (g_t[...].astype(F32) * inverse).astype(BF16)
        g_t[...] = shrunk
        gs[...] = shrunk.T
        delta = jnp.sum(
            attended_t.astype(F32) * shrunk.astype(F32), axis=0, keepdims=True
        )
        acc[...] = jnp.zeros_like(acc)

        def backward(at, count, carried):
            rows = rows_of(at, count)
            step = SLOPE // SPAN
            for c in range(count // step):
                d_prob = jnp.dot(
                    load(rows[c * step:(c + 1) * step], 1), g_t[...], preferred_element_type=F32
                )
                weight = weights[keys(at, c * SLOPE, SLOPE), :].astype(F32)
                d_scores[c * SLOPE:(c + 1) * SLOPE, :] = (weight * (d_prob - delta)).astype(BF16)
            acc[...] += lax.dot_general(
                load(rows, 0), d_scores[:count * SPAN, :], (((0,), (0,)), ((), ())),
                preferred_element_type=F32,
            )
            for c in range(count // PER_SUM):
                part = slice(c * PER_SUM * SPAN, (c + 1) * PER_SUM * SPAN)
                dk = jnp.dot(d_scores[part, :], qs[...], preferred_element_type=F32)
                dv = jnp.dot(
                    weights[keys(at, c * PER_SUM * SPAN, PER_SUM * SPAN), :], gs[...],
                    preferred_element_type=F32,
                )
                for b, r in enumerate(rows[c * PER_SUM:(c + 1) * PER_SUM]):
                    for column, terms in enumerate((dk, dv)):
                        place = (pl.ds(r, SPAN), slice(column * D, (column + 1) * D))
                        dkv_ref[place] = (
                            dkv_ref[place].astype(F32) + terms[b * SPAN:(b + 1) * SPAN, :]
                        ).astype(BF16)
            return carried

        tiles(backward, 0)
        dq = (acc[...] * SCALE).astype(BF16).T
        for h in range(HEADS):
            dq_ref[pl.ds(row, SPAN), h * D:(h + 1) * D] = dq[h * SPAN:(h + 1) * SPAN, :]
        return 0

    lax.fori_loop(0, 2, one_span, 0)


def attention(seq, order, seg, q, g, kv):
    return pl.pallas_call(
        attention_kernel,
        out_shape=(
            jax.ShapeDtypeStruct(q.shape, BF16),
            jax.ShapeDtypeStruct(q.shape, BF16),
            jax.ShapeDtypeStruct(kv.shape, BF16),
        ),
        in_specs=[SMEM, SMEM, VMEM, VMEM, VMEM, VMEM],
        out_specs=(VMEM, VMEM, VMEM),
        scratch_shapes=[
            pltpu.SMEM((SPANS,), jnp.int32),
            pltpu.VMEM((QROWS, D), BF16),
            pltpu.VMEM((QROWS, D), BF16),
            pltpu.VMEM((D, QROWS), BF16),
            pltpu.VMEM((D, QROWS), BF16),
            pltpu.VMEM((MOST_KEYS, QROWS), F32),
            pltpu.VMEM((MOST_KEYS, QROWS), BF16),
            pltpu.VMEM((max(SIZES) * UNIT * SPAN, QROWS), BF16),
            pltpu.VMEM((D, QROWS), F32),
        ],
        compiler_params=pltpu.CompilerParams(vmem_limit_bytes=ATTENTION_VMEM),
        name="attention",
    )(seq, order, seg, q, g, kv)


SUM_ROWS = 32
SPLIT = 64
FAR_FIRST = (4, 3, -3, 2, -2, 1, -1, 0)
UPWARD = (4, -3, 2, -1)
Z_SLOTS = 36


def scatter_kernel(
    part_ref, sum_ref, mine, theirs, landed, load_sem, send_sem, recv_sem, mate_send, mate_recv
):
    me = Place()
    y, z = me.y, me.z
    mate = me.device(core=1 - me.core)

    def of_z(s):
        return (slice(None),) + me.dz(s)[1:]

    def load_z(s):
        return pltpu.make_async_copy(
            part_ref.at[of_z(s) + (0,)], mine.at[of_z(s)], load_sem.at[me.dz(s)[0]]
        )

    def load_y(s):
        py = me.dy(s)
        return pltpu.make_async_copy(part_ref.at[py, :, :, 1], mine.at[py], load_sem.at[py])

    @pl.when(me.core == 0)
    def _():
        for s in FAR_FIRST:
            load_z(s).start()

    @pl.when(me.core == 1)
    def _():
        for s in (2, 1, -1, 0):
            load_y(s).start()

    me.greet(
        [mate]
        + [me.device(y=me.dy(s)) for s in (1, -1, 2)]
        + [me.device(z=me.dz(s)) for s in (1, -1, 2, -2)]
    )
    up_z, down_z = me.device(z=me.dz(1)), me.device(z=me.dz(-1))
    up_2z, down_2z = me.device(z=me.dz(2)), me.device(z=me.dz(-2))
    up_y, down_y = me.device(y=me.dy(1)), me.device(y=me.dy(-1))
    index = FAR_FIRST.index

    def keep(at, rows, total):
        mine[at + (rows,)] = total.astype(BF16)

    def write(at, rows, total):
        sum_ref[rows, :] = total

    class Route:
        def __init__(self, sends, start, size, first_sem):
            self.sends, self.start, self.size, self.first_sem = sends, start, size, first_sem

        def slot(self, slot):
            return landed.at[slot, pl.ds(self.start, self.size)]

        def terms(self, py, pz, slots, store):
            at = (py,) + pz[1:]
            for slot in slots:
                arrived(
                    self.slot(slot), mate_send.at[0], recv_sem.at[self.first_sem + slot], mate
                )

            def add(step, _):
                first = pl.multiple_of(self.start + step * SUM_ROWS, SUM_ROWS)
                rows = pl.ds(first, SUM_ROWS)
                total = mine[at + (rows,)].astype(F32) + theirs[at + (rows,)].astype(F32)
                for slot in slots:
                    total = total + landed[slot, rows].astype(F32)
                store(at, rows, total)
                return 0

            lax.fori_loop(0, self.size // SUM_ROWS, add, 0)
            return at

        def pass_on(self, py, pz, slots, slot, device):
            at = self.terms(py, pz, slots, keep)
            self.sends(
                mine.at[at + (pl.ds(self.start, self.size),)], self.slot(slot),
                recv_sem.at[self.first_sem + slot], device,
            )

    def y_far(route, s):
        device = up_y if s in UPWARD else down_y
        route.pass_on(me.dy(2), me.dz(s), (), index(s), device)

    def y_near(route, s):
        got = (index(s),)
        up, down = (got, ()) if s in UPWARD else ((), got)
        route.pass_on(me.dy(1), me.dz(s), up, 8 + index(s), up_y)
        route.pass_on(me.dy(-1), me.dz(s), down, 16 + index(s), down_y)

    def along_z(route, s):
        extra, device = {
            4: ((), up_2z), 3: ((), up_z), -3: ((), down_z), 2: ((3, 4), up_2z),
            -2: ((-3,), down_2z), 1: ((), up_z), -1: ((), down_z),
        }[s]
        got = (8 + index(s), 16 + index(s)) + tuple(24 + index(e) for e in extra)
        route.pass_on(y, me.dz(s), got, 24 + index(s), device)

    def y_last(route):
        got = (15, 23) + tuple(24 + index(e) for e in (1, -1, 2, -2))
        route.terms(y, z, got, write)

    @pl.when(me.core == 0)
    def _():
        sends = Sends(send_sem)
        mate_sends = Sends(mate_send)
        by_z = Route(sends, 0, SPLIT, 0)
        by_y = Route(sends, SPLIT, ROWS - SPLIT, Z_SLOTS)
        for s in FAR_FIRST:
            at = (me.dy(2),) + me.dz(s)[1:]
            mate_sends(
                part_ref.at[at + (1,)], theirs.at[at], mate_recv.at[4 + index(s)], mate
            )
        for s in (1, -1, 0):
            py = me.dy(s)
            mate_sends(part_ref.at[py, :, :, 1], theirs.at[py], mate_recv.at[py], mate)

        def ready(s):
            load_z(s).wait()
            arrived(theirs.at[of_z(s)], mate_send.at[0], mate_recv.at[me.dz(s)[0]], mate)

        order = (0, 1, -1, 2)
        up_slot = lambda s, i: (s - 1) * 4 + order.index(i)
        down_slot = lambda s, i: 16 + (s - 1) * 4 + order.index(i)

        def z_step(s):
            for i in order:
                got = (up_slot(s + 1, i),) if s < 3 else ()
                got += (up_slot(4, i),) if s == 2 and i in (0, 1) else ()
                by_z.pass_on(me.dy(i), me.dz(s), got, up_slot(s, i), up_z)
                got = (down_slot(s + 1, i),) if s < 3 else ()
                got += (down_slot(4, i),) if s == 2 and i in (-1, 2) else ()
                by_z.pass_on(me.dy(i), me.dz(-s), got, down_slot(s, i), down_z)

        ready(4)
        y_far(by_y, 4)
        for i in (0, -1, 1, 2):
            if i in (0, 1):
                by_z.pass_on(me.dy(i), me.dz(4), (), up_slot(4, i), up_2z)
            else:
                by_z.pass_on(me.dy(i), me.dz(4), (), down_slot(4, i), down_2z)
        for s in (3, -3):
            ready(s)
            y_far(by_y, s)
        z_step(3)
        for s in (2, -2):
            ready(s)
            y_far(by_y, s)
        for s in (4, 3, -3):
            y_near(by_y, s)
        z_step(2)
        for s in (1, -1, 0):
            ready(s)
            y_far(by_y, s)
        for s in (2, -2):
            y_near(by_y, s)
        for s in (4, 3, -3):
            along_z(by_y, s)
        z_step(1)
        for s in (1, -1, 0):
            y_near(by_y, s)
        for s in (2, -2):
            along_z(by_y, s)
        last = lambda i: (up_slot(1, i), down_slot(1, i))
        for i in (1, -1, 2):
            by_z.pass_on(me.dy(i), z, last(i), 32 + order.index(i), me.device(y=me.dy(i)))
        for s in (1, -1):
            along_z(by_y, s)
        by_z.terms(y, z, last(0) + (33, 34, 35), write)
        y_last(by_y)
        mate_sends.wait()
        sends.wait()

    @pl.when(me.core == 1)
    def _():
        sends = Sends(send_sem)
        mate_sends = Sends(mate_send)
        by_y = Route(sends, 0, ROWS, Z_SLOTS)
        for s in FAR_FIRST:
            at = of_z(s)
            mate_sends(part_ref.at[at + (0,)], theirs.at[at], mate_recv.at[me.dz(s)[0]], mate)

        def ready(s):
            py = me.dy(s)
            load_y(s).wait()
            arrived(theirs.at[py], mate_send.at[0], mate_recv.at[py], mate)

        load_y(2).wait()
        for s in FAR_FIRST:
            at = (me.dy(2),) + me.dz(s)[1:]
            arrived(theirs.at[at], mate_send.at[0], mate_recv.at[4 + index(s)], mate)
            y_far(by_y, s)
        ready(1)
        ready(-1)
        for s in FAR_FIRST[:6]:
            y_near(by_y, s)
        ready(0)
        for s in (4, 3, -3):
            along_z(by_y, s)
        for s in FAR_FIRST[6:]:
            y_near(by_y, s)
        for s in FAR_FIRST[3:-1]:
            along_z(by_y, s)
        y_last(by_y)
        mate_sends.wait()
        sends.wait()


def scatter(part):
    return pl.pallas_call(
        scatter_kernel,
        out_shape=jax.ShapeDtypeStruct((ROWS, 2 * D), F32),
        in_specs=[ANY],
        out_specs=VMEM,
        scratch_shapes=[
            pltpu.VMEM((4, 2, 4, ROWS, 2 * D), BF16),
            pltpu.VMEM((4, 2, 4, ROWS, 2 * D), BF16),
            pltpu.VMEM((36, ROWS, 2 * D), BF16),
            pltpu.SemaphoreType.DMA((8,)),
            pltpu.SemaphoreType.DMA((64,)),
            pltpu.SemaphoreType.DMA((Z_SLOTS + 32,)),
            pltpu.SemaphoreType.DMA((12,)),
            pltpu.SemaphoreType.DMA((12,)),
        ],
        compiler_params=pltpu.CompilerParams(
            collective_id=1, has_side_effects=True, vmem_limit_bytes=SCATTER_VMEM
        ),
        name="scatter",
    )(part)


def finish_kernel(sum_ref, dk_ref, dv_ref):
    dk_ref[...] = (sum_ref[:, :D] * SCALE).astype(BF16)
    dv_ref[...] = sum_ref[:, D:].astype(BF16)


def finish(sums):
    return pl.pallas_call(
        finish_kernel,
        out_shape=(jax.ShapeDtypeStruct((ROWS, D), BF16),) * 2,
        in_specs=[VMEM],
        out_specs=(VMEM, VMEM),
        compiler_params=pltpu.CompilerParams(vmem_limit_bytes=2 * MIB),
        name="finish",
    )(sums)


def shards(
    query_matrix, key_matrix, value_matrix, segment_ids, block_order, out_weight, d_attended
):
    seq = lax.axis_index(("inner", "outer")).astype(jnp.int32).reshape(1)
    pieces, g = gather(key_matrix, value_matrix, d_attended, out_weight)
    attended, d_queries, terms = attention(
        seq, block_order, segment_ids.reshape(64, 128), query_matrix, g,
        pieces.reshape(TOKENS, 2 * D),
    )
    sums = scatter(terms.reshape(PIECES))
    key_gradient, value_gradient = finish(sums)
    return (attended, d_queries, key_gradient, value_gradient)


def solution(mesh):
    return jax.shard_map(
        shards,
        mesh=mesh,
        in_specs=(
            P(("inner", "outer"), "tensor"),
            P(("inner", "outer"), "tensor"),
            P(("inner", "outer"), "tensor"),
            P(),
            P(),
            P("tensor", None),
            P(("inner", "outer", "tensor"), None),
        ),
        out_specs=(
            P(("inner", "outer"), "tensor"),
            P(("inner", "outer"), "tensor"),
            P(("inner", "outer"), "tensor"),
            P(("inner", "outer"), "tensor"),
        ),
        check_vma=False,
    )
```
